128 devices in a mesh: node: 8 (over z, core), local: 16 (over y, x).
Axes of the slice: x: 4, y: 4, z: 4, core: 2. Of those that a mesh axis runs over, the one named last changes fastest.
Arguments:
- tokens: bfloat16 [16384, 3584], P(('node', 'local')), may hold values from -6 to 6
- expert_ids: int32 [16384, 8], P(('node', 'local')), may hold values from 0 to 127, as said below
- combine_weights: bfloat16 [16384, 8], P(('node', 'local')), may hold values from 0.049804688 to 0.59765625
- gate_weight: bfloat16 [128, 3584, 1024], P(('node', 'local')), may hold values from -0.09375 to 0.09375
- up_weight: bfloat16 [128, 3584, 1024], P(('node', 'local')), may hold values from -0.09375 to 0.09375
- down_weight: bfloat16 [128, 1024, 3584], P(('node', 'local')), may hold values from -0.1875 to 0.1875
- latent_rows: bfloat16 [16384, 576], P(('node', 'local')), may hold values from -6 to 6
- latent_owner: int32 [16384], P(('node', 'local')), may hold values from 0 to 127, as said below
Outputs:
- moe_out: bfloat16 [16384, 3584], P(('node', 'local'))
- latent_cache: bfloat16 [16384, 576], P(('node', 'local'))
The draws below stay inside these ranges and needn't reach their ends.
Inputs may be any that keep to these rules, and one draw needn't show every extreme that they name: `expert_ids`: each token names 8 different experts, 2 on each of exactly 4 different nodes, where expert e lies on node e // 16. Of the tokens of one device, exactly 64 reach each node. Among the tokens of all devices that share one local index and reach one node, each expert of that node is named at most 80 times, and some experts are named exactly 80 times. `latent_owner`: devices are numbered node-major. Each device sends either no rows or exactly 2 rows to each owner, and each owner receives exactly 128 rows.
All inputs are finite; a program needn't handle non-finite values.
Results may differ from the reference program's by a relative error of at most 0.0064.
Values may be sent and summed in bfloat16 or wider, within the bound.
A program may use at most 128 MiB of HBM per device.

```python
import math
import jax
import jax.numpy as jnp
from jax import lax

D = 3584
FF = 1024
LATENT = 576
TOPK = 8
NODES_MAX = 4
LAT_CAP = 2
TOK_DEV = 128
EXPERTS = 128
PER_NODE = 2
CAP = 80
TOKENS = 16384
LAT_DEV = 128
LAT_ROWS = 16384
N_NODE = 8
N_LOCAL = 16


def draw_expert_ids(key, part):
    key = jax.random.fold_in(key, 11)
    key_rank, key_label, key_group, key_heat = jax.random.split(key, 4)
    device_count = N_NODE * N_LOCAL
    node_slots = TOK_DEV * NODES_MAX // N_NODE
    group_size = N_NODE * node_slots
    mean_load = PER_NODE * group_size // N_LOCAL
    ranks = jax.vmap(lambda k: jax.random.permutation(k, TOK_DEV))(jax.random.split(key_rank, device_count)).astype(jnp.int32)
    labels = jax.vmap(lambda k: jax.random.permutation(k, N_NODE))(jax.random.split(key_label, device_count)).astype(jnp.int32)
    group_order = jax.vmap(lambda k: jax.random.permutation(k, group_size))(jax.random.split(key_group, N_LOCAL * N_NODE)).astype(jnp.int32)
    group_order = group_order.reshape(N_LOCAL, N_NODE, group_size)
    heat = jax.vmap(lambda k: jax.random.permutation(k, N_LOCAL))(jax.random.split(key_heat, N_NODE)).astype(jnp.int32)
    loads = jnp.where(heat < N_LOCAL // 2, mean_load + mean_load // 4, mean_load - mean_load // 4)
    bounds = jnp.cumsum(loads, axis=1).astype(jnp.int32)
    ranks = ranks.reshape(N_NODE, N_LOCAL, TOK_DEV)
    labels = labels.reshape(N_NODE, N_LOCAL, N_NODE)
    pick_range = jnp.arange(NODES_MAX, dtype=jnp.int32)
    slot_pos = ranks[:, :, :, None] + pick_range * TOK_DEV
    label_index = slot_pos // node_slots
    within = slot_pos % node_slots
    node_of = jnp.take_along_axis(labels, label_index.reshape(N_NODE, N_LOCAL, -1), axis=2).reshape(slot_pos.shape)
    source_node = jnp.arange(N_NODE, dtype=jnp.int32)[:, None, None, None]
    local_index = jnp.arange(N_LOCAL, dtype=jnp.int32)[None, :, None, None]
    member = source_node * node_slots + within
    spot = group_order[local_index, node_of, member]
    positions = spot[..., None] + jnp.arange(PER_NODE, dtype=jnp.int32) * group_size
    node_bounds = bounds[node_of]
    expert_local = jnp.sum((node_bounds[..., None, :] <= positions[..., None]).astype(jnp.int32), axis=-1)
    ids = node_of[..., None] * N_LOCAL + expert_local
    return ids.reshape(TOKENS, TOPK).astype(jnp.int32)


def draw_latent_owner(key, part):
    key = jax.random.fold_in(key, 23)
    key_offset, key_rows = jax.random.split(key)
    device_count = N_NODE * N_LOCAL
    targets = LAT_DEV // LAT_CAP
    scores = jax.random.permutation(key_offset, device_count).astype(jnp.int32)
    offset_range = jnp.arange(device_count, dtype=jnp.int32)
    needed = (offset_range == 1) | (offset_range == device_count - 1) | (offset_range == device_count // 2) | (offset_range == N_LOCAL)
    scores = jnp.where(needed, scores - device_count, scores)
    offsets = jnp.argsort(scores, stable=True).astype(jnp.int32)[:targets]
    arrange = jax.vmap(lambda k: jax.random.permutation(k, LAT_DEV))(jax.random.split(key_rows, device_count)).astype(jnp.int32)
    source = jnp.arange(device_count, dtype=jnp.int32)[:, None]
    owner = (source + offsets[arrange // LAT_CAP]) % device_count
    return owner.reshape(LAT_ROWS).astype(jnp.int32)


def level_of(own_key, shape, pieces, smallest, high):
    def one(axis_at, parts):
        draws = jax.random.uniform(jax.random.fold_in(jax.random.fold_in(own_key, 6), axis_at), (parts,), jnp.float32, smallest / len(pieces), high / len(pieces))
        return jnp.repeat(jnp.exp(draws), shape[axis_at] // parts).reshape((-1,) + (1,) * (len(shape) - axis_at - 1))

    gain = one(*pieces[0])
    for cut in pieces[1:]:
        gain = gain * one(*cut)
    return gain


def gaussian(own_key, extent, spread, reach, cuts=(), kind=jnp.bfloat16):
    loudness = level_of(own_key, extent, cuts, -0.22, 0.18) if cuts else 1.0
    values = jax.random.normal(own_key, extent, jnp.float32) * spread * loudness
    return jnp.minimum(jnp.maximum(values, -reach), reach).astype(kind)


def setup_inputs(seed: int = 0) -> dict:
    key_list = jax.random.split(jax.random.key(seed), 9)
    return {
        "tokens": gaussian(key_list[0], (TOKENS, D), 1.0, 6.0, ((0, 128),)),
        "expert_ids": draw_expert_ids(jax.random.fold_in(key_list[8], 71), 0),
        "combine_weights": jnp.clip(jnp.exp(math.log(0.59765625) - 2.4849066 * jax.random.uniform(key_list[2], (TOKENS, TOPK), jnp.float32) ** level_of(key_list[2], (TOKENS, TOPK), ((0, 128),), -0.2, 0.2)), 0.049804688, 0.59765625).astype(jnp.bfloat16),
        "gate_weight": gaussian(key_list[3], (EXPERTS, D, FF), D ** -0.5, 0.09375, ((0, 128),)),
        "up_weight": gaussian(key_list[4], (EXPERTS, D, FF), D ** -0.5, 0.09375, ((0, 128),)),
        "down_weight": gaussian(key_list[5], (EXPERTS, FF, D), FF ** -0.5, 0.1875, ((0, 128),)),
        "latent_rows": gaussian(key_list[6], (LAT_ROWS, LATENT), 1.0, 6.0, ((0, 128),)),
        "latent_owner": draw_latent_owner(jax.random.fold_in(key_list[8], 71), 0),
    }


def reference(tokens, expert_ids, combine_weights, gate_weight, up_weight, down_weight, latent_rows, latent_owner):
    flat_ids = expert_ids.reshape(-1).astype(jnp.int32)
    flat_gates = combine_weights.reshape(-1).astype(jnp.float32)
    bound = N_LOCAL * CAP
    order = jnp.argsort(flat_ids, stable=True).astype(jnp.int32)
    order = jnp.concatenate([order, jnp.zeros((bound,), jnp.int32)])
    counts = jnp.bincount(flat_ids, length=EXPERTS).astype(jnp.int32)
    starts = (jnp.cumsum(counts) - counts).astype(jnp.int32)
    slot_range = jnp.arange(bound, dtype=jnp.int32)

    def expert_pass(expert, accum):
        pair = lax.dynamic_slice(order, (starts[expert],), (bound,))
        valid = slot_range < counts[expert]
        token_index = (pair // TOPK).astype(jnp.int32)
        rows = tokens[token_index]
        gate_act = jnp.dot(rows, gate_weight[expert], preferred_element_type=jnp.float32)
        up_act = jnp.dot(rows, up_weight[expert], preferred_element_type=jnp.float32)
        hidden = (jax.nn.silu(gate_act) * up_act).astype(jnp.bfloat16)
        result = jnp.dot(hidden, down_weight[expert], preferred_element_type=jnp.float32).astype(jnp.bfloat16)
        scale = jnp.where(valid, flat_gates[pair], jnp.zeros((), jnp.float32))
        return accum.at[token_index].add(scale[:, None] * result.astype(jnp.float32))

    def node_pass(node, summed):
        start = (node * N_LOCAL).astype(jnp.int32)
        accum = lax.fori_loop(start, start + N_LOCAL, expert_pass, jnp.zeros((TOKENS, D), jnp.float32))
        rounded = lax.optimization_barrier(accum.astype(jnp.bfloat16))
        return summed + rounded.astype(jnp.float32)

    summed = lax.fori_loop(jnp.int32(0), jnp.int32(N_NODE), node_pass, jnp.zeros((TOKENS, D), jnp.float32))
    moe_out = summed.astype(jnp.bfloat16)
    lat_order = jnp.argsort(latent_owner, stable=True).astype(jnp.int32)
    latent_cache = latent_rows[lat_order]
    return moe_out, latent_cache
```

```python
import functools

import jax
import jax.numpy as jnp
from jax import lax
from jax.experimental import pallas as pl
from jax.experimental.pallas import tpu as pltpu
from jax.sharding import PartitionSpec as P

MESH = pl.DeviceIdType.MESH
BF16 = jnp.bfloat16
F32 = jnp.float32

NODES = 8
LOCALS = 16
SIDE = 4
CAP = 80
NODE_ROWS = 64
TOK = 128
ROWS = NODES * NODE_ROWS
SLOTS = LOCALS * CAP
WIDTH = 512
TX_SLOTS = 3
LAT_PAD = 640


def iota(shape, dim):
    return lax.broadcasted_iota(jnp.int32, shape, dim)


def mm(a, b):
    return jnp.dot(a, b, preferred_element_type=F32)


def ones_where(mask):
    return jnp.where(mask, 1.0, 0.0)


def wait_for(ref, sem):
    pltpu.make_async_copy(ref, ref, sem).wait()


def rows_at(index, size):
    return pl.ds(pl.multiple_of(index * size, size), size)


def kernel(
    chunks,
    tok,
    ids_t,
    weights_t,
    lat,
    owner,
    wg,
    wu,
    wd,
    moe,
    latent_cache,
    choose,
    choose_t,
    gate_out,
    gate_in,
    pick,
    combine,
    zs,
    zr,
    tx,
    rx,
    ret,
    back,
    acc_gate,
    acc_up,
    hidden,
    wg_buf,
    wu_buf,
    wd_buf,
    lat_s1,
    lat_r1,
    lat_s2,
    lat_r2,
    sem_w,
    sem_z,
    sem_x,
    sem_ret,
    sem_back,
    sem_misc,
):
    node = lax.axis_index("node")
    local = lax.axis_index("local")
    z, core = node // 2, lax.rem(node, 2)
    y, x = local // SIDE, lax.rem(local, SIDE)

    def node_peer(d):
        dz, dc = d // 2, lax.rem(d, 2)
        return lax.rem(z + dz, SIDE) * 2 + lax.rem(core + dc, 2)

    def local_peer(d):
        dy, dx = d // SIDE, lax.rem(d, SIDE)
        return lax.rem(y + dy, SIDE) * SIDE + lax.rem(x + dx, SIDE)

    def to_nodes(src, dst, size, send_sem, recv_sem):
        @pl.loop(1, NODES)
        def _(d):
            peer = node_peer(d)
            pltpu.make_async_remote_copy(
                src_ref=src.at[rows_at(peer, size)],
                dst_ref=dst.at[rows_at(node, size)],
                send_sem=send_sem,
                recv_sem=recv_sem,
                device_id=(peer, local),
                device_id_type=MESH,
            ).start()

    def to_locals(src, dst, size, send_sem, recv_sem):
        @pl.loop(1, LOCALS)
        def _(d):
            peer = local_peer(d)
            pltpu.make_async_remote_copy(
                src_ref=src.at[rows_at(peer, size)],
                dst_ref=dst.at[rows_at(local, size)],
                send_sem=send_sem,
                recv_sem=recv_sem,
                device_id=(node, peer),
                device_id_type=MESH,
            ).start()

    def weights_in(k):
        cols = pl.ds(pl.multiple_of(k * WIDTH, WIDTH), WIDTH)
        slot = lax.rem(k, 2)
        return (
            pltpu.make_async_copy(wg.at[0, cols], wg_buf.at[slot], sem_w.at[0, slot]),
            pltpu.make_async_copy(wu.at[0, cols], wu_buf.at[slot], sem_w.at[1, slot]),
        )

    def down_in(k):
        cols = pl.ds(pl.multiple_of(k * WIDTH, WIDTH), WIDTH)
        slot = lax.rem(k, 2)
        return pltpu.make_async_copy(wd.at[0, :, cols], wd_buf.at[slot], sem_w.at[2, slot])

    barrier = pltpu.get_barrier_semaphore()

    @pl.loop(1, NODES)
    def _(d):
        pl.semaphore_signal(barrier, inc=1, device_id=(node_peer(d), local), device_id_type=MESH)

    @pl.loop(1, LOCALS)
    def _(d):
        pl.semaphore_signal(barrier, inc=1, device_id=(node, local_peer(d)), device_id_type=MESH)

    for copy in weights_in(0) + weights_in(1):
        copy.start()
    down_in(0).start()
    down_in(1).start()

    gates_t = jnp.zeros((TOK, TOK), F32)
    expert_row = iota((TOK, TOK), 0)
    for k in range(ids_t.shape[0]):
        gates_t += jnp.where(ids_t[k : k + 1, :] == expert_row, weights_t[k : k + 1, :], 0.0)
    gates = jnp.transpose(gates_t).astype(BF16)
    hit_t = ones_where(gates_t > 0.0).astype(BF16)
    upto = ones_where(iota((TOK, TOK), 0) <= iota((TOK, TOK), 1)).astype(BF16)
    of_node = ones_where((iota((ROWS, TOK), 0) >> 6) == (iota((ROWS, TOK), 1) >> 4)).astype(BF16)
    reached = ones_where(mm(of_node, hit_t) > 0.0)
    rank = mm(reached.astype(BF16), upto)
    slot_in_node = ((iota((ROWS, TOK), 0) & (NODE_ROWS - 1)) + 1).astype(F32)
    chosen = jnp.where(rank == slot_in_node, reached, 0.0)
    choose[...] = chosen.astype(BF16)
    gate_out[...] = mm(choose[...], gates).astype(BF16)

    pl.semaphore_wait(barrier, NODES - 1 + LOCALS - 1)

    to_nodes(gate_out, gate_in, NODE_ROWS, sem_misc.at[0], sem_misc.at[1])
    gate_in[rows_at(node, NODE_ROWS), :] = gate_out[rows_at(node, NODE_ROWS), :]

    @pl.loop(0, chunks)
    def _(k):
        cols = pl.ds(pl.multiple_of(k * WIDTH, WIDTH), WIDTH)
        zs[k] = mm(choose[...], tok[:, cols]).astype(BF16)
        to_nodes(zs.at[k], zr.at[k], NODE_ROWS, sem_z.at[0, k], sem_z.at[1, k])
        zr[k, rows_at(node, NODE_ROWS), :] = zs[k, rows_at(node, NODE_ROWS), :]

    lat_rows = LOCALS * NODES * 2
    row = iota((lat_rows, TOK), 0)
    owner_of_row = (((row & 15) >> 1) << 4) + (row >> 4)
    owned = ones_where(owner[...] == owner_of_row)
    owned_rank = mm(owned.astype(BF16), upto)
    lat_pick = jnp.where(owned_rank == ((row & 1) + 1).astype(F32), owned, 0.0).astype(BF16)
    lat_s1[...] = mm(lat_pick, lat[...]).astype(BF16)
    to_locals(lat_s1, lat_r1, 16, sem_misc.at[2], sem_misc.at[3])
    lat_r1[rows_at(local, 16), :] = lat_s1[rows_at(local, 16), :]

    choose_t[...] = jnp.transpose(chosen).astype(BF16)

    wait_for(gate_in.at[pl.ds(0, (NODES - 1) * NODE_ROWS)], sem_misc.at[1])
    got = gate_in[...].astype(F32)
    routed = ones_where(got > 0.0)
    before = ones_where(iota((ROWS, ROWS), 1) <= iota((ROWS, ROWS), 0)).astype(BF16)
    count = mm(before, routed.astype(BF16))
    count = jnp.where(routed > 0.0, jnp.minimum(count, 255.0), 0.0).astype(BF16)
    tile = 256

    @pl.loop(0, SLOTS // tile)
    def _(i):
        slot = iota((TOK, tile), 1) + i * tile
        first = (iota((TOK, tile), 0) - node * LOCALS) * CAP
        spread = ones_where((slot >= first) & (slot < first + CAP)).astype(BF16)
        gate_at = mm(gate_in[...], spread)
        count_at = mm(count, spread)
        slot_in_expert = lax.rem(iota((8, tile), 1) + i * tile, CAP)[0:1, :] + 1
        weight = jnp.where(count_at == slot_in_expert.astype(F32), gate_at, 0.0)
        combine[i] = weight.astype(BF16)
        pick[rows_at(i, tile), :] = jnp.transpose(ones_where(weight > 0.0)).astype(BF16)

    def expert_in(k):
        wait_for(rx.at[k, pl.ds(0, SLOTS - CAP)], sem_x.at[1, k])
        for copy in weights_in(k):
            copy.wait()
        slot = lax.rem(k, 2)

        @pl.loop(0, SLOTS // tile)
        def _(i):
            rows = rows_at(i, tile)
            part = rx[k, rows, :]

            @pl.when(k == 0)
            def _():
                acc_gate[rows, :] = mm(part, wg_buf[slot])
                acc_up[rows, :] = mm(part, wu_buf[slot])

            @pl.when(k > 0)
            def _():
                acc_gate[rows, :] += mm(part, wg_buf[slot])
                acc_up[rows, :] += mm(part, wu_buf[slot])

        @pl.when(k + 2 < chunks)
        def _():
            for copy in weights_in(k + 2):
                copy.start()

    @pl.loop(0, chunks + 1)
    def _(k):
        @pl.when(k < chunks)
        def _():
            slot = lax.rem(k, TX_SLOTS)
            wait_for(zr.at[k, pl.ds(0, (NODES - 1) * NODE_ROWS)], sem_z.at[1, k])

            @pl.when(k >= TX_SLOTS)
            def _():
                wait_for(tx.at[slot, pl.ds(0, SLOTS - CAP)], sem_x.at[0, k - TX_SLOTS])

            @pl.loop(0, SLOTS // tile)
            def _(i):
                rows = rows_at(i, tile)
                tx[slot, rows, :] = mm(pick[rows, :], zr[k]).astype(BF16)

            to_locals(tx.at[slot], rx.at[k], CAP, sem_x.at[0, k], sem_x.at[1, k])
            rx[k, rows_at(local, CAP), :] = tx[slot, rows_at(local, CAP), :]

        @pl.when(k >= 1)
        def _():
            expert_in(k - 1)

    wait_for(lat_r1.at[pl.ds(0, lat_rows - 16)], sem_misc.at[3])
    row = iota((lat_rows, lat_rows), 0)
    source = (((row & 31) >> 1) << 4) + ((row >> 5) << 1) + (row & 1)
    turn = ones_where(iota((lat_rows, lat_rows), 1) == source).astype(BF16)
    lat_s2[...] = mm(turn, lat_r1[...]).astype(BF16)
    to_nodes(lat_s2, lat_r2, 32, sem_misc.at[4], sem_misc.at[5])
    lat_r2[rows_at(node, 32), :] = lat_s2[rows_at(node, 32), :]

    @pl.loop(0, SLOTS // tile)
    def _(i):
        rows = rows_at(i, tile)
        gate_act = acc_gate[rows, :]
        hidden[rows, :] = (gate_act / (1.0 + jnp.exp(-gate_act)) * acc_up[rows, :]).astype(BF16)

    @pl.loop(0, chunks)
    def _(k):
        wait_for(zs.at[k, pl.ds(0, (NODES - 1) * NODE_ROWS)], sem_z.at[0, k])

    @pl.loop(chunks - TX_SLOTS, chunks)
    def _(k):
        wait_for(tx.at[0, pl.ds(0, SLOTS - CAP)], sem_x.at[0, k])

    def node_part(k):
        wait_for(ret.at[k, pl.ds(0, SLOTS - CAP)], sem_ret.at[1, k])
        total = mm(combine[0], ret[k, 0:tile, :])
        for i in range(1, SLOTS // tile):
            total += mm(combine[i], ret[k, i * tile : (i + 1) * tile, :])
        zs[k] = total.astype(BF16)
        to_nodes(zs.at[k], back.at[k], NODE_ROWS, sem_back.at[0, k], sem_back.at[1, k])
        back[k, rows_at(node, NODE_ROWS), :] = zs[k, rows_at(node, NODE_ROWS), :]

    def finish(k):
        wait_for(back.at[k, pl.ds(0, (NODES - 1) * NODE_ROWS)], sem_back.at[1, k])
        cols = pl.ds(pl.multiple_of(k * WIDTH, WIDTH), WIDTH)
        moe[:, cols] = mm(choose_t[...], back[k]).astype(BF16)

    @pl.loop(0, chunks + 2)
    def _(k):
        @pl.when(k < chunks)
        def _():
            slot = lax.rem(k, 2)
            down_in(k).wait()

            @pl.loop(0, SLOTS // tile)
            def _(i):
                rows = rows_at(i, tile)
                rx[k, rows, :] = mm(hidden[rows, :], wd_buf[slot]).astype(BF16)

            to_locals(rx.at[k], ret.at[k], CAP, sem_ret.at[0, k], sem_ret.at[1, k])
            ret[k, rows_at(local, CAP), :] = rx[k, rows_at(local, CAP), :]

            @pl.when(k + 2 < chunks)
            def _():
                down_in(k + 2).start()

        @pl.when((k >= 1) & (k < chunks + 1))
        def _():
            node_part(k - 1)

        @pl.when(k >= 2)
        def _():
            finish(k - 2)

    wait_for(lat_r2.at[pl.ds(0, lat_rows - 32)], sem_misc.at[5])
    arrived = lat_r2[...]
    mark = ones_where(iota((8, LAT_PAD), 1) == latent_cache.shape[1]).astype(BF16)
    live = lax.dot_general(mark, arrived, (((1,), (1,)), ((), ())), preferred_element_type=F32)
    upto_lat = ones_where(iota((lat_rows, lat_rows), 0) <= iota((lat_rows, lat_rows), 1))
    place = mm(live.astype(BF16), upto_lat.astype(BF16))
    wanted = (iota((TOK, lat_rows), 0) + 1).astype(F32)
    settle = jnp.where(place[0:1, :] == wanted, live[0:1, :], 0.0).astype(BF16)
    settled = mm(settle, arrived).astype(BF16)
    latent_cache[...] = settled[:, : latent_cache.shape[1]]

    @pl.loop(0, chunks)
    def _(k):
        wait_for(rx.at[k, pl.ds(0, SLOTS - CAP)], sem_ret.at[0, k])
        wait_for(zs.at[k, pl.ds(0, (NODES - 1) * NODE_ROWS)], sem_back.at[0, k])

    wait_for(gate_out.at[pl.ds(0, (NODES - 1) * NODE_ROWS)], sem_misc.at[0])
    wait_for(lat_s1.at[pl.ds(0, lat_rows - 16)], sem_misc.at[2])
    wait_for(lat_s2.at[pl.ds(0, lat_rows - 32)], sem_misc.at[4])


def per_device(tokens, ids, weights, wg, wu, wd, latent_rows, latent_owner):
    count, width = tokens.shape
    lat_width = latent_rows.shape[1]
    hidden_width = wg.shape[2]
    chunks = width // WIDTH
    lat = jnp.concatenate(
        [
            latent_rows,
            jnp.ones((count, 1), BF16),
            jnp.zeros((count, LAT_PAD - lat_width - 1), BF16),
        ],
        axis=1,
    )
    vmem = pl.BlockSpec(memory_space=pltpu.VMEM)
    hbm = pl.BlockSpec(memory_space=pl.ANY)
    lat_all = LOCALS * NODES * 2
    dma = pltpu.SemaphoreType.DMA
    return pl.pallas_call(
        functools.partial(kernel, chunks),
        out_shape=(
            jax.ShapeDtypeStruct((count, width), BF16),
            jax.ShapeDtypeStruct((count, lat_width), BF16),
        ),
        in_specs=[vmem] * 5 + [hbm] * 3,
        out_specs=(vmem, vmem),
        scratch_shapes=[
            pltpu.VMEM((ROWS, TOK), BF16),
            pltpu.VMEM((TOK, ROWS), BF16),
            pltpu.VMEM((ROWS, TOK), BF16),
            pltpu.VMEM((ROWS, TOK), BF16),
            pltpu.VMEM((SLOTS, ROWS), BF16),
            pltpu.VMEM((SLOTS // 256, ROWS, 256), BF16),
            pltpu.VMEM((chunks, ROWS, WIDTH), BF16),
            pltpu.VMEM((chunks, ROWS, WIDTH), BF16),
            pltpu.VMEM((TX_SLOTS, SLOTS, WIDTH), BF16),
            pltpu.VMEM((chunks, SLOTS, WIDTH), BF16),
            pltpu.VMEM((chunks, SLOTS, WIDTH), BF16),
            pltpu.VMEM((chunks, ROWS, WIDTH), BF16),
            pltpu.VMEM((SLOTS, hidden_width), F32),
            pltpu.VMEM((SLOTS, hidden_width), F32),
            pltpu.VMEM((SLOTS, hidden_width), BF16),
            pltpu.VMEM((2, WIDTH, hidden_width), BF16),
            pltpu.VMEM((2, WIDTH, hidden_width), BF16),
            pltpu.VMEM((2, hidden_width, WIDTH), BF16),
            pltpu.VMEM((lat_all, LAT_PAD), BF16),
            pltpu.VMEM((lat_all, LAT_PAD), BF16),
            pltpu.VMEM((lat_all, LAT_PAD), BF16),
            pltpu.VMEM((lat_all, LAT_PAD), BF16),
            dma((3, 2)),
            dma((2, chunks)),
            dma((2, chunks)),
            dma((2, chunks)),
            dma((2, chunks)),
            dma((6,)),
        ],
        compiler_params=pltpu.CompilerParams(
            collective_id=0, has_side_effects=True, vmem_limit_bytes=62 * 2**20
        ),
        cost_estimate=pl.CostEstimate(
            flops=6 * SLOTS * width * hidden_width,
            bytes_accessed=6 * width * hidden_width,
            transcendentals=SLOTS * hidden_width,
        ),
        name="moe_exchange",
    )(
        tokens,
        jnp.transpose(ids),
        jnp.transpose(weights).astype(F32),
        lat,
        latent_owner.reshape(1, count),
        wg,
        wu,
        wd,
    )


def solution(mesh):
    rows = P(("node", "local"), None)
    experts = P(("node", "local"), None, None)
    return jax.shard_map(
        per_device,
        mesh=mesh,
        in_specs=(rows, rows, rows, experts, experts, experts, rows, P(("node", "local"))),
        out_specs=(rows, rows),
        check_vma=False,
    )
```

```python
import functools

import jax
import jax.numpy as jnp
from jax import lax
from jax.experimental import pallas as pl
from jax.experimental.pallas import tpu as pltpu
from jax.sharding import PartitionSpec as P

MESH = pl.DeviceIdType.MESH
BF16 = jnp.bfloat16
F32 = jnp.float32

NODES = 8
LOCALS = 16
SIDE = 4
CAP = 80
NODE_ROWS = 64
TOK = 128
ROWS = NODES * NODE_ROWS
SLOTS = LOCALS * CAP
GROUP = SIDE * CAP
WIDTH = 256
TX_SLOTS = 4
AHEAD = 4
EXPERT_LAG = 2
PART_LAG = 3
HOME_LAG = 5
STRIDE = 3
LAT_PAD = 640


def iota(shape, dim):
    return lax.broadcasted_iota(jnp.int32, shape, dim)


def mm(a, b):
    return jnp.dot(a, b, preferred_element_type=F32)


def mm_nt(a, b):
    return lax.dot_general(a, b, (((1,), (1,)), ((), ())), preferred_element_type=F32)


def ones_where(mask):
    return jnp.where(mask, 1.0, 0.0)


def wait_for(ref, sem):
    pltpu.make_async_copy(ref, ref, sem).wait()


def rows_at(index, size):
    return pl.ds(pl.multiple_of(index * size, size), size)


def kernel(
    chunks,
    tok,
    ids_t,
    weights_t,
    lat_t,
    owner,
    wg,
    wu,
    wd,
    moe,
    latent_cache,
    choose,
    choose_t,
    gate_out,
    gate_in,
    pick,
    combine,
    zs,
    zr,
    tx,
    rx,
    ret,
    back,
    acc_gate,
    acc_up,
    hidden,
    wg_buf,
    wu_buf,
    wd_buf,
    lat_pad,
    lat_s1,
    lat_r1,
    lat_s2,
    lat_r2,
    sem_w,
    sem_z,
    sem_tx,
    sem_rx,
    sem_ret,
    sem_back,
    sem_misc,
):
    node = lax.axis_index("node")
    local = lax.axis_index("local")
    z, core = node // 2, lax.rem(node, 2)
    y, x = local // SIDE, lax.rem(local, SIDE)

    def node_peer(d):
        dz, dc = d // 2, lax.rem(d, 2)
        return lax.rem(z + dz, SIDE) * 2 + lax.rem(core + dc, 2)

    def local_peer(d):
        dy, dx = d // SIDE, lax.rem(d, SIDE)
        return lax.rem(y + dy, SIDE) * SIDE + lax.rem(x + dx, SIDE)

    def to_nodes(src, dst, size, send_sem, recv_sem):
        @pl.loop(1, NODES)
        def _(d):
            peer = node_peer(d)
            pltpu.make_async_remote_copy(
                src_ref=src.at[rows_at(peer, size)],
                dst_ref=dst.at[rows_at(node, size)],
                send_sem=send_sem,
                recv_sem=recv_sem,
                device_id=(peer, local),
                device_id_type=MESH,
            ).start()

    def to_locals(src, dst, size, send_sem, recv_sem):
        @pl.loop(1, LOCALS)
        def _(d):
            peer = local_peer(lax.rem(d * STRIDE, LOCALS))
            pltpu.make_async_remote_copy(
                src_ref=src.at[rows_at(peer, size)],
                dst_ref=dst.at[rows_at(local, size)],
                send_sem=send_sem,
                recv_sem=recv_sem,
                device_id=(node, peer),
                device_id_type=MESH,
            ).start()

    def send_rows(k, slot):
        @pl.loop(1, LOCALS)
        def _(d):
            turn = lax.rem(d * STRIDE, LOCALS)
            peer = local_peer(turn)
            pltpu.make_async_remote_copy(
                src_ref=tx.at[slot, rows_at(peer, CAP)],
                dst_ref=rx.at[k, rows_at(local, CAP)],
                send_sem=sem_tx.at[k],
                recv_sem=sem_rx.at[k, lax.rem(SIDE - turn // SIDE, SIDE)],
                device_id=(node, peer),
                device_id_type=MESH,
            ).start()

    def wait_group(k, g):
        @pl.when(g == 0)
        def _():
            wait_for(rx.at[k, pl.ds(0, GROUP - CAP)], sem_rx.at[k, g])

        @pl.when(g > 0)
        def _():
            wait_for(rx.at[k, pl.ds(0, GROUP)], sem_rx.at[k, g])

    def weights_in(k):
        cols = pl.ds(pl.multiple_of(k * WIDTH, WIDTH), WIDTH)
        slot = lax.rem(k, 2)
        return (
            pltpu.make_async_copy(wg.at[0, cols], wg_buf.at[slot], sem_w.at[0, slot]),
            pltpu.make_async_copy(wu.at[0, cols], wu_buf.at[slot], sem_w.at[1, slot]),
        )

    def down_in(k):
        cols = pl.ds(pl.multiple_of(k * WIDTH, WIDTH), WIDTH)
        slot = lax.rem(k, 2)
        return pltpu.make_async_copy(wd.at[0, :, cols], wd_buf.at[slot], sem_w.at[2, slot])

    barrier = pltpu.get_barrier_semaphore()

    @pl.loop(1, NODES)
    def _(d):
        pl.semaphore_signal(barrier, inc=1, device_id=(node_peer(d), local), device_id_type=MESH)

    @pl.loop(1, LOCALS)
    def _(d):
        pl.semaphore_signal(barrier, inc=1, device_id=(node, local_peer(d)), device_id_type=MESH)

    for copy in weights_in(0) + weights_in(1):
        copy.start()
    down_in(0).start()
    down_in(1).start()

    given = weights_t[...].astype(F32)
    gates_t = jnp.zeros((TOK, TOK), F32)
    expert_row = iota((TOK, TOK), 0)
    for k in range(ids_t.shape[0]):
        gates_t += jnp.where(ids_t[k : k + 1, :] == expert_row, given[k : k + 1, :], 0.0)
    gates = jnp.transpose(gates_t).astype(BF16)
    hit_t = ones_where(gates_t > 0.0).astype(BF16)
    upto = ones_where(iota((TOK, TOK), 0) <= iota((TOK, TOK), 1)).astype(BF16)
    of_node = ones_where((iota((ROWS, TOK), 0) >> 6) == (iota((ROWS, TOK), 1) >> 4)).astype(BF16)
    reached = ones_where(mm(of_node, hit_t) > 0.0)
    rank = mm(reached.astype(BF16), upto)
    slot_in_node = ((iota((ROWS, TOK), 0) & (NODE_ROWS - 1)) + 1).astype(F32)
    chosen = jnp.where(rank == slot_in_node, reached, 0.0)
    choose[...] = chosen.astype(BF16)
    gate_out[...] = mm(choose[...], gates).astype(BF16)

    pl.semaphore_wait(barrier, NODES - 1 + LOCALS - 1)

    to_nodes(gate_out, gate_in, NODE_ROWS, sem_misc.at[0], sem_misc.at[1])
    gate_in[rows_at(node, NODE_ROWS), :] = gate_out[rows_at(node, NODE_ROWS), :]

    def node_send(k):
        cols = pl.ds(pl.multiple_of(k * WIDTH, WIDTH), WIDTH)
        zs[k] = mm(choose[...], tok[:, cols]).astype(BF16)
        to_nodes(zs.at[k], zr.at[k], NODE_ROWS, sem_z.at[0, k], sem_z.at[1, k])
        zr[k, rows_at(node, NODE_ROWS), :] = zs[k, rows_at(node, NODE_ROWS), :]

    @pl.loop(0, AHEAD)
    def _(k):
        node_send(k)

    choose_t[...] = jnp.transpose(chosen).astype(BF16)

    wait_for(gate_in.at[pl.ds(0, (NODES - 1) * NODE_ROWS)], sem_misc.at[1])
    got = gate_in[...].astype(F32)
    routed = ones_where(got > 0.0)
    before = ones_where(iota((ROWS, ROWS), 1) <= iota((ROWS, ROWS), 0)).astype(BF16)
    count = mm(before, routed.astype(BF16))
    count = jnp.where(routed > 0.0, jnp.minimum(count, 255.0), 0.0).astype(BF16)
    tile = 256

    @pl.loop(0, SLOTS // tile)
    def _(i):
        slot = iota((TOK, tile), 1) + i * tile
        first = (iota((TOK, tile), 0) - node * LOCALS) * CAP
        spread = ones_where((slot >= first) & (slot < first + CAP)).astype(BF16)
        gate_at = mm(gate_in[...], spread)
        count_at = mm(count, spread)
        slot_in_expert = lax.rem(iota((8, tile), 1) + i * tile, CAP)[0:1, :] + 1
        weight = jnp.where(count_at == slot_in_expert.astype(F32), gate_at, 0.0)
        combine[i] = weight.astype(BF16)
        pick[rows_at(i, tile), :] = jnp.transpose(ones_where(weight > 0.0)).astype(BF16)

    lat_rows = LOCALS * NODES * 2

    def latent_first():
        width = latent_cache.shape[0]
        lat_pad[0:width, :] = lat_t[...]
        lat_pad[width:, :] = ones_where(iota((LAT_PAD - width, TOK), 0) == 0).astype(BF16)
        row = iota((lat_rows, TOK), 0)
        owner_of_row = (((row & 15) >> 1) << 4) + (row >> 4)
        owned = ones_where(owner[...] == owner_of_row)
        upto = ones_where(iota((TOK, TOK), 0) <= iota((TOK, TOK), 1)).astype(BF16)
        rank = mm(owned.astype(BF16), upto)
        lat_pick = jnp.where(rank == ((row & 1) + 1).astype(F32), owned, 0.0).astype(BF16)
        lat_s1[...] = mm_nt(lat_pick, lat_pad[...]).astype(BF16)
        to_locals(lat_s1, lat_r1, 16, sem_misc.at[2], sem_misc.at[3])
        lat_r1[rows_at(local, 16), :] = lat_s1[rows_at(local, 16), :]

    def latent_second():
        wait_for(lat_r1.at[pl.ds(0, lat_rows - 16)], sem_misc.at[3])
        row = iota((lat_rows, lat_rows), 0)
        source = (((row & 31) >> 1) << 4) + ((row >> 5) << 1) + (row & 1)
        turn = ones_where(iota((lat_rows, lat_rows), 1) == source).astype(BF16)
        lat_s2[...] = mm(turn, lat_r1[...]).astype(BF16)
        to_nodes(lat_s2, lat_r2, 32, sem_misc.at[4], sem_misc.at[5])
        lat_r2[rows_at(node, 32), :] = lat_s2[rows_at(node, 32), :]

    def latent_third():
        wait_for(lat_r2.at[pl.ds(0, lat_rows - 32)], sem_misc.at[5])
        arrived = lat_r2[...]
        mark = ones_where(iota((8, LAT_PAD), 1) == latent_cache.shape[0]).astype(BF16)
        live = mm_nt(mark, arrived)
        upto = ones_where(iota((lat_rows, lat_rows), 0) <= iota((lat_rows, lat_rows), 1))
        place = mm(live.astype(BF16), upto.astype(BF16))
        wanted = (iota((TOK, lat_rows), 0) + 1).astype(F32)
        settle = jnp.where(place[0:1, :] == wanted, live[0:1, :], 0.0).astype(BF16)
        settled = jnp.transpose(mm(settle, arrived))
        latent_cache[...] = settled[0 : latent_cache.shape[0], :].astype(BF16)

    def expert_in(k):
        for copy in weights_in(k):
            copy.wait()
        slot = lax.rem(k, 2)

        @pl.loop(0, SIDE)
        def _(g):
            wait_group(k, g)
            rows = rows_at(lax.rem(y + g, SIDE), GROUP)
            part = rx[k, rows, :]

            @pl.when(k == 0)
            def _():
                acc_gate[rows, :] = mm(part, wg_buf[slot])
                acc_up[rows, :] = mm(part, wu_buf[slot])

            @pl.when(k > 0)
            def _():
                acc_gate[rows, :] += mm(part, wg_buf[slot])
                acc_up[rows, :] += mm(part, wu_buf[slot])

        @pl.when(k + 2 < chunks)
        def _():
            for copy in weights_in(k + 2):
                copy.start()

    def expert_rows(k):
        slot = lax.rem(k, TX_SLOTS)
        wait_for(zr.at[k, pl.ds(0, (NODES - 1) * NODE_ROWS)], sem_z.at[1, k])

        @pl.when(k >= TX_SLOTS)
        def _():
            wait_for(tx.at[slot, pl.ds(0, SLOTS - CAP)], sem_tx.at[k - TX_SLOTS])

        @pl.loop(0, SLOTS // tile)
        def _(i):
            rows = rows_at(i, tile)
            tx[slot, rows, :] = mm(pick[rows, :], zr[k]).astype(BF16)

        send_rows(k, slot)
        rx[k, rows_at(local, CAP), :] = tx[slot, rows_at(local, CAP), :]

    @pl.loop(0, chunks - 1 + EXPERT_LAG)
    def _(k):
        @pl.when(k < chunks)
        def _():
            expert_rows(k)

        @pl.when(k + AHEAD < chunks)
        def _():
            node_send(k + AHEAD)

        @pl.when(k == 1)
        def _():
            latent_first()

        @pl.when(k == 6)
        def _():
            latent_second()

        @pl.when(k >= EXPERT_LAG)
        def _():
            expert_in(k - EXPERT_LAG)

    last = chunks - 1
    for copy in weights_in(last):
        copy.wait()
    down_in(0).wait()

    @pl.loop(0, SIDE)
    def _(g):
        wait_group(last, g)
        there = lax.rem(y + g, SIDE)
        rows = rows_at(there, GROUP)
        part = rx[last, rows, :]
        gate_act = acc_gate[rows, :] + mm(part, wg_buf[last % 2])
        up_act = acc_up[rows, :] + mm(part, wu_buf[last % 2])
        hidden[rows, :] = (gate_act / (1.0 + jnp.exp(-gate_act)) * up_act).astype(BF16)
        rx[0, rows, :] = mm(hidden[rows, :], wd_buf[0]).astype(BF16)

        @pl.loop(0, SIDE)
        def _(dx):
            peer = there * SIDE + lax.rem(x + dx, SIDE)

            @pl.when(g + dx > 0)
            def _():
                pltpu.make_async_remote_copy(
                    src_ref=rx.at[0, rows_at(peer, CAP)],
                    dst_ref=ret.at[0, rows_at(local, CAP)],
                    send_sem=sem_ret.at[0, 0],
                    recv_sem=sem_ret.at[1, 0],
                    device_id=(node, peer),
                    device_id_type=MESH,
                ).start()

    ret[0, rows_at(local, CAP), :] = rx[0, rows_at(local, CAP), :]
    down_in(2).start()

    @pl.loop(0, chunks)
    def _(k):
        wait_for(zs.at[k, pl.ds(0, (NODES - 1) * NODE_ROWS)], sem_z.at[0, k])

    @pl.loop(chunks - TX_SLOTS, chunks)
    def _(k):
        wait_for(tx.at[0, pl.ds(0, SLOTS - CAP)], sem_tx.at[k])

    def node_part(k):
        wait_for(ret.at[k, pl.ds(0, SLOTS - CAP)], sem_ret.at[1, k])
        total = mm(combine[0], ret[k, 0:tile, :])
        for i in range(1, SLOTS // tile):
            total += mm(combine[i], ret[k, i * tile : (i + 1) * tile, :])
        zs[k] = total.astype(BF16)
        to_nodes(zs.at[k], back.at[k], NODE_ROWS, sem_back.at[0, k], sem_back.at[1, k])
        back[k, rows_at(node, NODE_ROWS), :] = zs[k, rows_at(node, NODE_ROWS), :]

    def finish(k):
        wait_for(back.at[k, pl.ds(0, (NODES - 1) * NODE_ROWS)], sem_back.at[1, k])
        cols = pl.ds(pl.multiple_of(k * WIDTH, WIDTH), WIDTH)
        moe[:, cols] = mm(choose_t[...], back[k]).astype(BF16)

    @pl.loop(1, chunks + HOME_LAG)
    def _(k):
        @pl.when(k < chunks)
        def _():
            slot = lax.rem(k, 2)
            down_in(k).wait()

            @pl.loop(0, SIDE)
            def _(i):
                rows = rows_at(i, GROUP)
                rx[k, rows, :] = mm(hidden[rows, :], wd_buf[slot]).astype(BF16)

            to_locals(rx.at[k], ret.at[k], CAP, sem_ret.at[0, k], sem_ret.at[1, k])
            ret[k, rows_at(local, CAP), :] = rx[k, rows_at(local, CAP), :]

            @pl.when(k + 2 < chunks)
            def _():
                down_in(k + 2).start()

        @pl.when((k >= PART_LAG) & (k < chunks + PART_LAG))
        def _():
            node_part(k - PART_LAG)

        @pl.when(k == 6)
        def _():
            latent_third()

        @pl.when(k >= HOME_LAG)
        def _():
            finish(k - HOME_LAG)

    @pl.loop(0, chunks)
    def _(k):
        wait_for(rx.at[k, pl.ds(0, SLOTS - CAP)], sem_ret.at[0, k])
        wait_for(zs.at[k, pl.ds(0, (NODES - 1) * NODE_ROWS)], sem_back.at[0, k])

    wait_for(gate_out.at[pl.ds(0, (NODES - 1) * NODE_ROWS)], sem_misc.at[0])
    wait_for(lat_s1.at[pl.ds(0, lat_rows - 16)], sem_misc.at[2])
    wait_for(lat_s2.at[pl.ds(0, lat_rows - 32)], sem_misc.at[4])


def per_device(tokens, ids, weights, wg, wu, wd, latent_rows, latent_owner):
    count, width = tokens.shape
    lat_width = latent_rows.shape[1]
    hidden_width = wg.shape[2]
    chunks = width // WIDTH
    vmem = pl.BlockSpec(memory_space=pltpu.VMEM)
    hbm = pl.BlockSpec(memory_space=pl.ANY)
    lat_all = LOCALS * NODES * 2
    dma = pltpu.SemaphoreType.DMA
    moe, cache_t = pl.pallas_call(
        functools.partial(kernel, chunks),
        out_shape=(
            jax.ShapeDtypeStruct((count, width), BF16),
            jax.ShapeDtypeStruct((lat_width, count), BF16),
        ),
        in_specs=[vmem] * 5 + [hbm] * 3,
        out_specs=(vmem, vmem),
        scratch_shapes=[
            pltpu.VMEM((ROWS, TOK), BF16),
            pltpu.VMEM((TOK, ROWS), BF16),
            pltpu.VMEM((ROWS, TOK), BF16),
            pltpu.VMEM((ROWS, TOK), BF16),
            pltpu.VMEM((SLOTS, ROWS), BF16),
            pltpu.VMEM((SLOTS // 256, ROWS, 256), BF16),
            pltpu.VMEM((chunks, ROWS, WIDTH), BF16),
            pltpu.VMEM((chunks, ROWS, WIDTH), BF16),
            pltpu.VMEM((TX_SLOTS, SLOTS, WIDTH), BF16),
            pltpu.VMEM((chunks, SLOTS, WIDTH), BF16),
            pltpu.VMEM((chunks, SLOTS, WIDTH), BF16),
            pltpu.VMEM((chunks, ROWS, WIDTH), BF16),
            pltpu.VMEM((SLOTS, hidden_width), F32),
            pltpu.VMEM((SLOTS, hidden_width), F32),
            pltpu.VMEM((SLOTS, hidden_width), BF16),
            pltpu.VMEM((2, WIDTH, hidden_width), BF16),
            pltpu.VMEM((2, WIDTH, hidden_width), BF16),
            pltpu.VMEM((2, hidden_width, WIDTH), BF16),
            pltpu.VMEM((LAT_PAD, count), BF16),
            pltpu.VMEM((lat_all, LAT_PAD), BF16),
            pltpu.VMEM((lat_all, LAT_PAD), BF16),
            pltpu.VMEM((lat_all, LAT_PAD), BF16),
            pltpu.VMEM((lat_all, LAT_PAD), BF16),
            dma((3, 2)),
            dma((2, chunks)),
            dma((chunks,)),
            dma((chunks, SIDE)),
            dma((2, chunks)),
            dma((2, chunks)),
            dma((6,)),
        ],
        compiler_params=pltpu.CompilerParams(
            collective_id=0, has_side_effects=True, vmem_limit_bytes=62 * 2**20
        ),
        cost_estimate=pl.CostEstimate(
            flops=6 * SLOTS * width * hidden_width,
            bytes_accessed=6 * width * hidden_width,
            transcendentals=SLOTS * hidden_width,
        ),
        name="moe_exchange",
    )(
        tokens,
        jnp.transpose(ids),
        jnp.transpose(weights),
        jnp.transpose(latent_rows),
        latent_owner.reshape(1, count),
        wg,
        wu,
        wd,
    )
    return moe, jnp.transpose(cache_t)


def solution(mesh):
    rows = P(("node", "local"), None)
    experts = P(("node", "local"), None, None)
    return jax.shard_map(
        per_device,
        mesh=mesh,
        in_specs=(rows, rows, rows, experts, experts, experts, rows, P(("node", "local"))),
        out_specs=(rows, rows),
        check_vma=False,
    )
```

```python
import functools

import jax
import jax.numpy as jnp
from jax import lax
from jax.experimental import pallas as pl
from jax.experimental.pallas import tpu as pltpu
from jax.sharding import PartitionSpec as P

MESH = pl.DeviceIdType.MESH
BF16 = jnp.bfloat16
F32 = jnp.float32

NODES = 8
LOCALS = 16
SIDE = 4
TYPES = 4
COVER = 8
CAP = 80
NODE_ROWS = 64
PAIR_ROWS = 2 * NODE_ROWS
TOK = 128
ROWS = NODES * NODE_ROWS
SLOTS = LOCALS * CAP
HALF = COVER * CAP
GROUP = SIDE * CAP
REMOTE = 2 * (COVER - 1)
WIDTH = 256
TX_SLOTS = 6
ZS_SLOTS = 4
AHEAD = 3
EXPERT_LAG = 4
PART_LAG = 5
HOME_LAG = 7
END_LAG = 8
STRIDE = 3
BUILD = 128
LAT_PAD = 640


def iota(shape, dim):
    return lax.broadcasted_iota(jnp.int32, shape, dim)


def mm(a, b):
    return jnp.dot(a, b, preferred_element_type=F32)


def mm_nt(a, b):
    return lax.dot_general(a, b, (((1,), (1,)), ((), ())), preferred_element_type=F32)


def ones_where(mask):
    return jnp.where(mask, 1.0, 0.0)


def wait_for(ref, sem):
    pltpu.make_async_copy(ref, ref, sem).wait()


def rows_at(index, size):
    return pl.ds(pl.multiple_of(index * size, size), size)


def kernel(
    chunks,
    tok,
    ids_t,
    weights_t,
    lat_t,
    owner,
    wg,
    wu,
    wd,
    moe,
    latent_cache,
    named,
    named_in,
    choose,
    choose_t,
    gates,
    counts,
    gate_out,
    moves,
    shared,
    shared_back,
    zs,
    passed,
    tx,
    rx,
    back,
    acc_gate,
    acc_up,
    hidden,
    wg_buf,
    wu_buf,
    wd_buf,
    lat_pad,
    lat_s1,
    lat_r1,
    lat_s2,
    lat_r2,
    sem_w,
    sem_named,
    sem_gates,
    sem_shared,
    sem_home,
    sem_z,
    sem_tx,
    sem_rx,
    sem_ret,
    sem_back,
    sem_misc,
):
    node = lax.axis_index("node")
    local = lax.axis_index("local")
    z, core = node // 2, lax.rem(node, 2)
    y, x = local // SIDE, lax.rem(local, SIDE)

    def node_peer(d):
        dz, dc = d // 2, lax.rem(d, 2)
        return lax.rem(z + dz, SIDE) * 2 + lax.rem(core + dc, 2)

    def local_peer(d):
        dy, dx = d // SIDE, lax.rem(d, SIDE)
        return lax.rem(y + dy, SIDE) * SIDE + lax.rem(x + dx, SIDE)

    def paired(v, way):
        return (1 - way) * (v + 1 - 2 * lax.rem(v, 2)) + way * (SIDE - 1 - v)

    def kind(k):
        t = lax.rem(k, TYPES)
        return lax.rem(t, 2), t // 2

    def partner_of(py, px, t):
        along_x, way = kind(t)
        return (
            py + (1 - along_x) * (paired(py, way) - py),
            px + along_x * (paired(px, way) - px),
        )

    def partner_at(t):
        py, px = partner_of(y, x, t)
        return py * SIDE + px

    def cover(t, a, b):
        along_x, way = kind(t)
        cy = (1 - along_x) * (y + a * (paired(y, 1 - way) - y)) + along_x * lax.rem(y + b, SIDE)
        cx = along_x * (x + a * (paired(x, 1 - way) - x)) + (1 - along_x) * lax.rem(x + b, SIDE)
        return cy, cx

    def send(src, dst, send_sem, recv_sem, device):
        pltpu.make_async_remote_copy(
            src_ref=src,
            dst_ref=dst,
            send_sem=send_sem,
            recv_sem=recv_sem,
            device_id=device,
            device_id_type=MESH,
        ).start()

    def to_nodes(src, dst, size, send_sem, recv_sem):
        @pl.loop(1, NODES)
        def _(d):
            peer = node_peer(d)
            send(
                src.at[rows_at(peer, size)],
                dst.at[rows_at(node, size)],
                send_sem,
                recv_sem,
                (peer, local),
            )

    def to_locals(src, dst, size, send_sem, recv_sem):
        @pl.loop(1, LOCALS)
        def _(d):
            peer = local_peer(lax.rem(d * STRIDE, LOCALS))
            send(
                src.at[rows_at(peer, size)],
                dst.at[rows_at(local, size)],
                send_sem,
                recv_sem,
                (node, peer),
            )

    def columns(k):
        return pl.ds(pl.multiple_of(k * WIDTH, WIDTH), WIDTH)

    def weights_in(k):
        slot = lax.rem(k, 2)
        return (
            pltpu.make_async_copy(wg.at[0, columns(k)], wg_buf.at[slot], sem_w.at[0, slot]),
            pltpu.make_async_copy(wu.at[0, columns(k)], wu_buf.at[slot], sem_w.at[1, slot]),
        )

    def down_in(k):
        slot = lax.rem(k, 2)
        return pltpu.make_async_copy(wd.at[0, :, columns(k)], wd_buf.at[slot], sem_w.at[2, slot])

    barrier = pltpu.get_barrier_semaphore()

    @pl.loop(1, LOCALS)
    def _(d):
        pl.semaphore_signal(barrier, inc=1, device_id=(node, local_peer(d)), device_id_type=MESH)

    @pl.loop(1, NODES)
    def _(d):
        pl.semaphore_signal(barrier, inc=1, device_id=(node_peer(d), local), device_id_type=MESH)

    for copy in weights_in(0) + weights_in(1):
        copy.start()
    down_in(0).start()
    down_in(1).start()
    named[0 : ids_t.shape[0], :] = ids_t[...].astype(F32)
    named[ids_t.shape[0] :, :] = weights_t[...].astype(F32)

    def route(who, names):
        gates_t = jnp.zeros((TOK, TOK), F32)
        expert_row = iota((TOK, TOK), 0).astype(F32)
        top = ids_t.shape[0]
        for k in range(top):
            hit = names[k : k + 1, :] == expert_row
            gates_t += jnp.where(hit, names[top + k : top + k + 1, :], 0.0)
        hit_t = ones_where(gates_t > 0.0).astype(BF16)
        upto = ones_where(iota((TOK, TOK), 0) <= iota((TOK, TOK), 1)).astype(BF16)
        of_node = ones_where((iota((ROWS, TOK), 0) >> 6) == (iota((ROWS, TOK), 1) >> 4))
        reached = ones_where(mm(of_node.astype(BF16), hit_t) > 0.0)
        rank = mm(reached.astype(BF16), upto)
        slot_in_node = ((iota((ROWS, TOK), 0) & (NODE_ROWS - 1)) + 1).astype(F32)
        choose[who] = jnp.where(rank == slot_in_node, reached, 0.0).astype(BF16)
        return gates_t

    own_gates = jnp.transpose(route(0, named[...])).astype(BF16)
    gate_out[...] = mm(choose[0], own_gates).astype(BF16)

    pl.semaphore_wait(barrier, NODES - 1 + LOCALS - 1)

    to_nodes(gate_out, gates.at[0], NODE_ROWS, sem_misc.at[0], sem_misc.at[1])

    @pl.loop(0, TYPES)
    def _(t):
        there = (node, partner_at(t))
        send(named, named_in.at[t], sem_named.at[0, t], sem_named.at[1, t], there)

    @pl.loop(0, chunks)
    def _(k):
        there = (node, partner_at(k))
        send(
            tok.at[:, columns(k)], shared.at[k], sem_shared.at[0, k], sem_shared.at[1, k], there
        )

    gates[0, rows_at(node, NODE_ROWS), :] = gate_out[rows_at(node, NODE_ROWS), :]

    def put_pair(slot, side, value):
        for n in range(NODES):
            at = n * PAIR_ROWS + side * NODE_ROWS
            zs[slot, at : at + NODE_ROWS, :] = value[n * NODE_ROWS : (n + 1) * NODE_ROWS, :]

    def get_pair(ref, k, side):
        starts = [n * PAIR_ROWS + side * NODE_ROWS for n in range(NODES)]
        return jnp.concatenate([ref[k, at : at + NODE_ROWS, :] for at in starts], axis=0)

    def node_send(k):
        t = lax.rem(k, TYPES)
        slot = lax.rem(k, ZS_SLOTS)

        @pl.when(k < TYPES)
        def _():
            wait_for(named_in.at[t], sem_named.at[1, t])
            route(1 + t, named_in[t])

        @pl.when(k >= ZS_SLOTS)
        def _():
            wait_for(zs.at[slot, pl.ds(0, (NODES - 1) * PAIR_ROWS)], sem_z.at[0, k - ZS_SLOTS])

        put_pair(slot, 0, mm(choose[0], tok[:, columns(k)]).astype(BF16))
        wait_for(shared.at[k], sem_shared.at[1, k])
        put_pair(slot, 1, mm(choose[1 + t], shared[k]).astype(BF16))
        to_nodes(zs.at[slot], passed.at[k], PAIR_ROWS, sem_z.at[0, k], sem_z.at[1, k])
        passed[k, rows_at(node, PAIR_ROWS), :] = zs[slot, rows_at(node, PAIR_ROWS), :]

    def count_rows(who):
        routed = ones_where(gates[who].astype(F32) > 0.0)
        before = ones_where(iota((ROWS, ROWS), 1) <= iota((ROWS, ROWS), 0)).astype(BF16)
        count = mm(before, routed.astype(BF16))
        counts[who] = jnp.where(routed > 0.0, jnp.minimum(count, 255.0), 0.0).astype(BF16)

    def expert_lane(slot, t):
        along_x, way = kind(t)
        i = lax.div(slot, CAP)
        a, b = i >> 2, i & 3
        on_y = y + a * (paired(y, 1 - way) - y)
        on_x = x + a * (paired(x, 1 - way) - x)
        lane_y = on_y * SIDE + ((x + b) & 3)
        lane_x = ((y + b) & 3) * SIDE + on_x
        return node * LOCALS + (1 - along_x) * lane_y + along_x * lane_x

    def build_pick(t):
        @pl.loop(0, 2 * HALF // BUILD)
        def _(j):
            side = j // (HALF // BUILD)
            i = lax.rem(j, HALF // BUILD)
            who = side * (1 + t)
            slot = iota((BUILD, TOK), 0) + i * BUILD
            spread = ones_where(iota((BUILD, TOK), 1) == expert_lane(slot, t)).astype(BF16)
            count_at = mm_nt(spread, counts[who])
            wanted = (lax.rem(iota((BUILD, ROWS), 0) + i * BUILD, CAP) + 1).astype(F32)
            moves[t, side, rows_at(i, BUILD), :] = ones_where(count_at == wanted).astype(BF16)

    def build_combine(t):
        @pl.loop(0, 2 * HALF // BUILD)
        def _(j):
            side = j // (HALF // BUILD)
            i = lax.rem(j, HALF // BUILD)
            who = side * (1 + t)
            slot = iota((TOK, BUILD), 1) + i * BUILD
            spread = ones_where(iota((TOK, BUILD), 0) == expert_lane(slot, t)).astype(BF16)
            count_at = mm(counts[who], spread)
            gate_at = mm(gates[who], spread)
            wanted = (lax.rem(iota((8, BUILD), 1) + i * BUILD, CAP)[0:1, :] + 1).astype(F32)
            weight = jnp.where(count_at == wanted, gate_at, 0.0).astype(BF16)
            for q in range(ROWS // BUILD):
                moves[t, side, rows_at(i, BUILD), q * BUILD : (q + 1) * BUILD] = weight[
                    q * BUILD : (q + 1) * BUILD, :
                ]

    node_send(0)
    wait_for(gates.at[0, pl.ds(0, (NODES - 1) * NODE_ROWS)], sem_misc.at[1])

    @pl.loop(0, TYPES)
    def _(t):
        there = (node, partner_at(t))
        send(gates.at[0], gates.at[1 + t], sem_gates.at[0, t], sem_gates.at[1, t], there)

    count_rows(0)

    @pl.loop(1, AHEAD)
    def _(k):
        node_send(k)

    lat_rows = LOCALS * NODES * 2

    def latent_first():
        width = latent_cache.shape[0]
        lat_pad[0:width, :] = lat_t[...]
        lat_pad[width:, :] = ones_where(iota((LAT_PAD - width, TOK), 0) == 0).astype(BF16)
        row = iota((lat_rows, TOK), 0)
        owner_of_row = (((row & 15) >> 1) << 4) + (row >> 4)
        owned = ones_where(owner[...] == owner_of_row)
        upto = ones_where(iota((TOK, TOK), 0) <= iota((TOK, TOK), 1)).astype(BF16)
        rank = mm(owned.astype(BF16), upto)
        lat_pick = jnp.where(rank == ((row & 1) + 1).astype(F32), owned, 0.0).astype(BF16)
        lat_s1[...] = mm_nt(lat_pick, lat_pad[...]).astype(BF16)
        to_locals(lat_s1, lat_r1, 16, sem_misc.at[2], sem_misc.at[3])
        lat_r1[rows_at(local, 16), :] = lat_s1[rows_at(local, 16), :]

    def latent_second():
        wait_for(lat_r1.at[pl.ds(0, lat_rows - 16)], sem_misc.at[3])
        row = iota((lat_rows, lat_rows), 0)
        source = (((row & 31) >> 1) << 4) + ((row >> 5) << 1) + (row & 1)
        turn = ones_where(iota((lat_rows, lat_rows), 1) == source).astype(BF16)
        lat_s2[...] = mm(turn, lat_r1[...]).astype(BF16)
        to_nodes(lat_s2, lat_r2, 32, sem_misc.at[4], sem_misc.at[5])
        lat_r2[rows_at(node, 32), :] = lat_s2[rows_at(node, 32), :]

    def latent_third():
        wait_for(lat_r2.at[pl.ds(0, lat_rows - 32)], sem_misc.at[5])
        arrived = lat_r2[...]
        mark = ones_where(iota((8, LAT_PAD), 1) == latent_cache.shape[0]).astype(BF16)
        live = mm_nt(mark, arrived)
        upto = ones_where(iota((lat_rows, lat_rows), 0) <= iota((lat_rows, lat_rows), 1))
        place = mm(live.astype(BF16), upto.astype(BF16))
        wanted = (iota((TOK, lat_rows), 0) + 1).astype(F32)
        settle = jnp.where(place[0:1, :] == wanted, live[0:1, :], 0.0).astype(BF16)
        settled = jnp.transpose(mm(settle, arrived))
        latent_cache[...] = settled[0 : latent_cache.shape[0], :].astype(BF16)

    def wait_group(k, cy):
        py, _ = partner_of(y, x, k)
        missing = (cy == y).astype(jnp.int32) + (cy == py).astype(jnp.int32)
        for skipped in range(3):

            @pl.when(missing == skipped)
            def _():
                wait_for(rx.at[k, pl.ds(0, GROUP - skipped * CAP)], sem_rx.at[k, cy])

    def expert_in(k):
        for copy in weights_in(k):
            copy.wait()
        slot = lax.rem(k, 2)

        @pl.loop(0, SIDE)
        def _(g):
            cy = lax.rem(y + g, SIDE)
            wait_group(k, cy)
            rows = rows_at(cy, GROUP)
            part = rx[k, rows, :]

            @pl.when(k == 0)
            def _():
                acc_gate[rows, :] = mm(part, wg_buf[slot])
                acc_up[rows, :] = mm(part, wu_buf[slot])

            @pl.when(k > 0)
            def _():
                acc_gate[rows, :] += mm(part, wg_buf[slot])
                acc_up[rows, :] += mm(part, wu_buf[slot])

        @pl.when(k + 2 < chunks)
        def _():
            for copy in weights_in(k + 2):
                copy.start()

    def expert_rows(k):
        t = lax.rem(k, TYPES)
        slot = lax.rem(k, TX_SLOTS)

        @pl.when(k < TYPES)
        def _():
            wait_for(gates.at[1 + t], sem_gates.at[1, t])
            count_rows(1 + t)
            build_pick(t)

        wait_for(passed.at[k, pl.ds(0, (NODES - 1) * PAIR_ROWS)], sem_z.at[1, k])

        @pl.when(k >= TX_SLOTS)
        def _():
            wait_for(tx.at[slot, pl.ds(0, REMOTE * CAP)], sem_tx.at[k - TX_SLOTS])

        for side in range(2):
            arrived = get_pair(passed, k, side)
            rows = pl.ds(side * HALF, HALF)
            tx[slot, rows, :] = mm(moves[t, side], arrived).astype(BF16)

        py, px = partner_of(y, x, k)

        @pl.loop(0, REMOTE)
        def _(m):
            side = m // (COVER - 1)
            i = 1 + lax.rem(m * STRIDE, COVER - 1)
            ey, ex = cover(k, i // SIDE, lax.rem(i, SIDE))
            cy = y + side * (py - y)
            cx = x + side * (px - x)
            send(
                tx.at[slot, rows_at(side * COVER + i, CAP)],
                rx.at[k, rows_at(cy * SIDE + cx, CAP)],
                sem_tx.at[k],
                sem_rx.at[k, cy],
                (node, ey * SIDE + ex),
            )

        rx[k, rows_at(local, CAP), :] = tx[slot, 0:CAP, :]
        rx[k, rows_at(py * SIDE + px, CAP), :] = tx[slot, HALF : HALF + CAP, :]

    @pl.loop(0, chunks - 1 + EXPERT_LAG)
    def _(k):
        @pl.when(k < chunks)
        def _():
            expert_rows(k)

        @pl.when(k + AHEAD < chunks)
        def _():
            node_send(k + AHEAD)

        @pl.when(k == 4)
        def _():
            latent_first()

        @pl.when(k == 8)
        def _():
            latent_second()

        @pl.when(k >= EXPERT_LAG)
        def _():
            expert_in(k - EXPERT_LAG)

    def send_back(k, a, b, side):
        fy, fx = cover(k, a, b)
        py, px = partner_of(fy, fx, k)
        cy = fy + side * (py - fy)
        cx = fx + side * (px - fx)
        i = a * SIDE + lax.rem(SIDE - b, SIDE)
        send(
            rx.at[k, rows_at(cy * SIDE + cx, CAP)],
            passed.at[k, rows_at(side * COVER + i, CAP)],
            sem_ret.at[0, k],
            sem_ret.at[1, k],
            (node, fy * SIDE + fx),
        )

    def keep_back(k):
        passed[k, 0:CAP, :] = rx[k, rows_at(local, CAP), :]
        passed[k, HALF : HALF + CAP, :] = rx[k, rows_at(partner_at(k), CAP), :]

    last = chunks - 1
    for copy in weights_in(last):
        copy.wait()
    down_in(0).wait()

    @pl.loop(0, SIDE)
    def _(g):
        a, side = lax.rem(g, 2), g // 2
        fy, fx = cover(0, a, 0)
        py, _ = partner_of(fy, fx, 0)
        there = fy + side * (py - fy)
        wait_group(last, there)
        rows = rows_at(there, GROUP)
        part = rx[last, rows, :]
        gate_act = acc_gate[rows, :] + mm(part, wg_buf[last % 2])
        up_act = acc_up[rows, :] + mm(part, wu_buf[last % 2])
        hidden[rows, :] = (gate_act / (1.0 + jnp.exp(-gate_act)) * up_act).astype(BF16)
        rx[0, rows, :] = mm(hidden[rows, :], wd_buf[0]).astype(BF16)

        @pl.loop(0, SIDE)
        def _(b):
            @pl.when(a + b > 0)
            def _():
                send_back(0, a, b, side)

    keep_back(0)
    down_in(2).start()

    @pl.loop(chunks - ZS_SLOTS, chunks)
    def _(k):
        wait_for(zs.at[0, pl.ds(0, (NODES - 1) * PAIR_ROWS)], sem_z.at[0, k])

    @pl.loop(chunks - TX_SLOTS, chunks)
    def _(k):
        wait_for(tx.at[0, pl.ds(0, REMOTE * CAP)], sem_tx.at[k])

    parts = [pl.ds(i * BUILD, BUILD) for i in range(HALF // BUILD)]

    def node_part(k):
        t = lax.rem(k, TYPES)
        slot = lax.rem(k, ZS_SLOTS)

        @pl.when(k < TYPES)
        def _():
            build_combine(t)

        wait_for(passed.at[k, pl.ds(0, REMOTE * CAP)], sem_ret.at[1, k])

        @pl.when(k >= ZS_SLOTS)
        def _():
            wait_for(zs.at[slot, pl.ds(0, (NODES - 1) * PAIR_ROWS)], sem_back.at[0, k - ZS_SLOTS])

        for side in range(2):
            weight = jnp.concatenate(
                [
                    jnp.concatenate(
                        [moves[t, side, part, pl.ds(q * BUILD, BUILD)] for part in parts], axis=1
                    )
                    for q in range(ROWS // BUILD)
                ],
                axis=0,
            )
            total = mm(weight, passed[k, side * HALF : (side + 1) * HALF, :])
            put_pair(slot, side, total.astype(BF16))

        to_nodes(zs.at[slot], back.at[k], PAIR_ROWS, sem_back.at[0, k], sem_back.at[1, k])
        back[k, rows_at(node, PAIR_ROWS), :] = zs[slot, rows_at(node, PAIR_ROWS), :]

    def to_partner(k):
        t = lax.rem(k, TYPES)

        @pl.when(k < TYPES)
        def _():
            choose_t[1 + t] = jnp.transpose(choose[1 + t].astype(F32)).astype(BF16)

        wait_for(back.at[k, pl.ds(0, (NODES - 1) * PAIR_ROWS)], sem_back.at[1, k])
        shared[k] = mm(choose_t[1 + t], get_pair(back, k, 1)).astype(BF16)
        there = (node, partner_at(k))
        send(shared.at[k], shared_back.at[k], sem_home.at[0, k], sem_home.at[1, k], there)

    def finish(k):
        own = mm(choose_t[0], get_pair(back, k, 0))
        wait_for(shared_back.at[k], sem_home.at[1, k])
        moe[:, columns(k)] = (own + shared_back[k].astype(F32)).astype(BF16)

    choose_t[0] = jnp.transpose(choose[0].astype(F32)).astype(BF16)

    @pl.loop(1, chunks + END_LAG)
    def _(k):
        @pl.when(k < chunks)
        def _():
            slot = lax.rem(k, 2)
            down_in(k).wait()

            @pl.loop(0, SIDE)
            def _(i):
                rows = rows_at(i, GROUP)
                rx[k, rows, :] = mm(hidden[rows, :], wd_buf[slot]).astype(BF16)

            @pl.loop(0, REMOTE)
            def _(m):
                j = 1 + lax.rem(m * STRIDE, COVER - 1)
                send_back(k, j // SIDE, lax.rem(j, SIDE), m // (COVER - 1))

            keep_back(k)

            @pl.when(k + 2 < chunks)
            def _():
                down_in(k + 2).start()

        @pl.when((k >= PART_LAG) & (k < chunks + PART_LAG))
        def _():
            node_part(k - PART_LAG)

        @pl.when(k == 9)
        def _():
            latent_third()

        @pl.when((k >= HOME_LAG) & (k < chunks + HOME_LAG))
        def _():
            to_partner(k - HOME_LAG)

        @pl.when(k >= END_LAG)
        def _():
            finish(k - END_LAG)

    @pl.loop(0, chunks)
    def _(k):
        wait_for(shared.at[k], sem_shared.at[0, k])
        wait_for(shared.at[k], sem_home.at[0, k])
        wait_for(rx.at[k, pl.ds(0, REMOTE * CAP)], sem_ret.at[0, k])

    @pl.loop(chunks - ZS_SLOTS, chunks)
    def _(k):
        wait_for(zs.at[0, pl.ds(0, (NODES - 1) * PAIR_ROWS)], sem_back.at[0, k])

    @pl.loop(0, TYPES)
    def _(t):
        wait_for(named, sem_named.at[0, t])
        wait_for(gates.at[0], sem_gates.at[0, t])

    wait_for(gate_out.at[pl.ds(0, (NODES - 1) * NODE_ROWS)], sem_misc.at[0])
    wait_for(lat_s1.at[pl.ds(0, lat_rows - 16)], sem_misc.at[2])
    wait_for(lat_s2.at[pl.ds(0, lat_rows - 32)], sem_misc.at[4])


def per_device(tokens, ids, weights, wg, wu, wd, latent_rows, latent_owner):
    count, width = tokens.shape
    lat_width = latent_rows.shape[1]
    hidden_width = wg.shape[2]
    chunks = width // WIDTH
    vmem = pl.BlockSpec(memory_space=pltpu.VMEM)
    hbm = pl.BlockSpec(memory_space=pl.ANY)
    lat_all = LOCALS * NODES * 2
    dma = pltpu.SemaphoreType.DMA
    moe, cache_t = pl.pallas_call(
        functools.partial(kernel, chunks),
        out_shape=(
            jax.ShapeDtypeStruct((count, width), BF16),
            jax.ShapeDtypeStruct((lat_width, count), BF16),
        ),
        in_specs=[vmem] * 5 + [hbm] * 3,
        out_specs=(vmem, vmem),
        scratch_shapes=[
            pltpu.VMEM((2 * ids.shape[1], TOK), F32),
            pltpu.VMEM((TYPES, 2 * ids.shape[1], TOK), F32),
            pltpu.VMEM((1 + TYPES, ROWS, TOK), BF16),
            pltpu.VMEM((1 + TYPES, TOK, ROWS), BF16),
            pltpu.VMEM((1 + TYPES, ROWS, TOK), BF16),
            pltpu.VMEM((1 + TYPES, ROWS, TOK), BF16),
            pltpu.VMEM((ROWS, TOK), BF16),
            pltpu.VMEM((TYPES, 2, HALF, ROWS), BF16),
            pltpu.VMEM((chunks, TOK, WIDTH), BF16),
            pltpu.VMEM((chunks, TOK, WIDTH), BF16),
            pltpu.VMEM((ZS_SLOTS, NODES * PAIR_ROWS, WIDTH), BF16),
            pltpu.VMEM((chunks, SLOTS, WIDTH), BF16),
            pltpu.VMEM((TX_SLOTS, SLOTS, WIDTH), BF16),
            pltpu.VMEM((chunks, SLOTS, WIDTH), BF16),
            pltpu.VMEM((chunks, NODES * PAIR_ROWS, WIDTH), BF16),
            pltpu.VMEM((SLOTS, hidden_width), F32),
            pltpu.VMEM((SLOTS, hidden_width), F32),
            pltpu.VMEM((SLOTS, hidden_width), BF16),
            pltpu.VMEM((2, WIDTH, hidden_width), BF16),
            pltpu.VMEM((2, WIDTH, hidden_width), BF16),
            pltpu.VMEM((2, hidden_width, WIDTH), BF16),
            pltpu.VMEM((LAT_PAD, count), BF16),
            pltpu.VMEM((lat_all, LAT_PAD), BF16),
            pltpu.VMEM((lat_all, LAT_PAD), BF16),
            pltpu.VMEM((lat_all, LAT_PAD), BF16),
            pltpu.VMEM((lat_all, LAT_PAD), BF16),
            dma((3, 2)),
            dma((2, TYPES)),
            dma((2, TYPES)),
            dma((2, chunks)),
            dma((2, chunks)),
            dma((2, chunks)),
            dma((chunks,)),
            dma((chunks, SIDE)),
            dma((2, chunks)),
            dma((2, chunks)),
            dma((6,)),
        ],
        compiler_params=pltpu.CompilerParams(
            collective_id=0, has_side_effects=True, vmem_limit_bytes=62 * 2**20
        ),
        cost_estimate=pl.CostEstimate(
            flops=6 * SLOTS * width * hidden_width,
            bytes_accessed=6 * width * hidden_width,
            transcendentals=SLOTS * hidden_width,
        ),
        name="moe_exchange",
    )(
        tokens,
        jnp.transpose(ids),
        jnp.transpose(weights),
        jnp.transpose(latent_rows),
        latent_owner.reshape(1, count),
        wg,
        wu,
        wd,
    )
    return moe, jnp.transpose(cache_t)


def solution(mesh):
    rows = P(("node", "local"), None)
    experts = P(("node", "local"), None, None)
    return jax.shard_map(
        per_device,
        mesh=mesh,
        in_specs=(rows, rows, rows, experts, experts, experts, rows, P(("node", "local"))),
        out_specs=(rows, rows),
        check_vma=False,
    )
```

```python
import functools

import jax
import jax.numpy as jnp
from jax import lax
from jax.experimental import pallas as pl
from jax.experimental.pallas import tpu as pltpu
from jax.sharding import PartitionSpec as P

MESH = pl.DeviceIdType.MESH
BF16 = jnp.bfloat16
F32 = jnp.float32

NODES = 8
LOCALS = 16
SIDE = 4
TYPES = 4
COVER = 8
CAP = 80
NODE_ROWS = 64
PAIR_ROWS = 2 * NODE_ROWS
TOK = 128
ROWS = NODES * NODE_ROWS
SLOTS = LOCALS * CAP
HALF = COVER * CAP
GROUP = SIDE * CAP
REMOTE = 2 * (COVER - 1)
WIDTH = 256
TX_SLOTS = 6
ZS_SLOTS = 4
AHEAD = 3
EXPERT_LAG = 4
PART_LAG = 5
HOME_LAG = 7
END_LAG = 8
FLAT_FIRST = 2
FLAT_LAST = 3
STRIDE = 3
BUILD = 128
LAT_PAD = 640


def iota(shape, dim):
    return lax.broadcasted_iota(jnp.int32, shape, dim)


def mm(a, b):
    return jnp.dot(a, b, preferred_element_type=F32)


def mm_nt(a, b):
    return lax.dot_general(a, b, (((1,), (1,)), ((), ())), preferred_element_type=F32)


def ones_where(mask):
    return jnp.where(mask, 1.0, 0.0)


def wait_for(ref, sem):
    pltpu.make_async_copy(ref, ref, sem).wait()


def rows_at(index, size):
    return pl.ds(pl.multiple_of(index * size, size), size)


def kernel(
    chunks,
    tok,
    ids_t,
    weights_t,
    lat_t,
    owner,
    wg,
    wu,
    wd,
    moe,
    latent_cache,
    named,
    named_in,
    choose,
    choose_t,
    gates,
    counts,
    gate_out,
    moves,
    shared,
    shared_back,
    zs,
    passed,
    tx,
    rx,
    back,
    acc_gate,
    acc_up,
    hidden,
    wg_buf,
    wu_buf,
    wd_buf,
    lat_pad,
    lat_s1,
    lat_r1,
    lat_s2,
    lat_r2,
    sem_w,
    sem_named,
    sem_gates,
    sem_shared,
    sem_home,
    sem_z,
    sem_tx,
    sem_rx,
    sem_ret,
    sem_back,
    sem_misc,
):
    node = lax.axis_index("node")
    local = lax.axis_index("local")
    z, core = node // 2, lax.rem(node, 2)
    y, x = local // SIDE, lax.rem(local, SIDE)

    def node_peer(d):
        dz, dc = d // 2, lax.rem(d, 2)
        return lax.rem(z + dz, SIDE) * 2 + lax.rem(core + dc, 2)

    def local_peer(d):
        dy, dx = d // SIDE, lax.rem(d, SIDE)
        return lax.rem(y + dy, SIDE) * SIDE + lax.rem(x + dx, SIDE)

    def paired(v, way):
        return (1 - way) * (v + 1 - 2 * lax.rem(v, 2)) + way * (SIDE - 1 - v)

    def kind(k):
        t = lax.rem(k, TYPES)
        return lax.rem(t, 2), t // 2

    def partner_of(py, px, t):
        along_x, way = kind(t)
        return (
            py + (1 - along_x) * (paired(py, way) - py),
            px + along_x * (paired(px, way) - px),
        )

    def partner_at(t):
        py, px = partner_of(y, x, t)
        return py * SIDE + px

    def cover(t, a, b):
        along_x, way = kind(t)
        cy = (1 - along_x) * (y + a * (paired(y, 1 - way) - y)) + along_x * lax.rem(y + b, SIDE)
        cx = along_x * (x + a * (paired(x, 1 - way) - x)) + (1 - along_x) * lax.rem(x + b, SIDE)
        return cy, cx

    def send(src, dst, send_sem, recv_sem, device):
        pltpu.make_async_remote_copy(
            src_ref=src,
            dst_ref=dst,
            send_sem=send_sem,
            recv_sem=recv_sem,
            device_id=device,
            device_id_type=MESH,
        ).start()

    def to_nodes(src, dst, size, send_sem, recv_sem):
        @pl.loop(1, NODES)
        def _(d):
            peer = node_peer(d)
            send(
                src.at[rows_at(peer, size)],
                dst.at[rows_at(node, size)],
                send_sem,
                recv_sem,
                (peer, local),
            )

    def to_locals(src, dst, size, send_sem, recv_sem):
        @pl.loop(1, LOCALS)
        def _(d):
            peer = local_peer(lax.rem(d * STRIDE, LOCALS))
            send(
                src.at[rows_at(peer, size)],
                dst.at[rows_at(local, size)],
                send_sem,
                recv_sem,
                (node, peer),
            )

    def columns(k):
        return pl.ds(pl.multiple_of(k * WIDTH, WIDTH), WIDTH)

    def weights_in(k):
        slot = lax.rem(k, 2)
        return (
            pltpu.make_async_copy(wg.at[0, columns(k)], wg_buf.at[slot], sem_w.at[0, slot]),
            pltpu.make_async_copy(wu.at[0, columns(k)], wu_buf.at[slot], sem_w.at[1, slot]),
        )

    def down_in(k):
        slot = lax.rem(k, 2)
        return pltpu.make_async_copy(wd.at[0, :, columns(k)], wd_buf.at[slot], sem_w.at[2, slot])

    barrier = pltpu.get_barrier_semaphore()

    @pl.loop(1, LOCALS)
    def _(d):
        pl.semaphore_signal(barrier, inc=1, device_id=(node, local_peer(d)), device_id_type=MESH)

    @pl.loop(1, NODES)
    def _(d):
        pl.semaphore_signal(barrier, inc=1, device_id=(node_peer(d), local), device_id_type=MESH)

    for copy in weights_in(0) + weights_in(1):
        copy.start()
    down_in(0).start()
    down_in(1).start()
    named[0 : ids_t.shape[0], :] = ids_t[...].astype(F32)
    named[ids_t.shape[0] :, :] = weights_t[...].astype(F32)

    def route(who, names):
        gates_t = jnp.zeros((TOK, TOK), F32)
        expert_row = iota((TOK, TOK), 0).astype(F32)
        top = ids_t.shape[0]
        for k in range(top):
            hit = names[k : k + 1, :] == expert_row
            gates_t += jnp.where(hit, names[top + k : top + k + 1, :], 0.0)
        hit_t = ones_where(gates_t > 0.0).astype(BF16)
        upto = ones_where(iota((TOK, TOK), 0) <= iota((TOK, TOK), 1)).astype(BF16)
        of_node = ones_where((iota((ROWS, TOK), 0) >> 6) == (iota((ROWS, TOK), 1) >> 4))
        reached = ones_where(mm(of_node.astype(BF16), hit_t) > 0.0)
        rank = mm(reached.astype(BF16), upto)
        slot_in_node = ((iota((ROWS, TOK), 0) & (NODE_ROWS - 1)) + 1).astype(F32)
        choose[who] = jnp.where(rank == slot_in_node, reached, 0.0).astype(BF16)
        return gates_t

    own_gates = jnp.transpose(route(0, named[...])).astype(BF16)
    gate_out[...] = mm(choose[0], own_gates).astype(BF16)

    pl.semaphore_wait(barrier, NODES - 1 + LOCALS - 1)

    to_nodes(gate_out, gates.at[0], NODE_ROWS, sem_misc.at[0], sem_misc.at[1])

    flat_back = chunks - FLAT_LAST

    def either(flat, ref, flat_rows, rows, sem):
        @pl.when(flat)
        def _():
            wait_for(ref.at[pl.ds(0, flat_rows)], sem)

        @pl.when(jnp.logical_not(flat))
        def _():
            wait_for(ref.at[pl.ds(0, rows)], sem)

    def wait_node_rows(flat, ref, sem):
        either(flat, ref, (NODES - 1) * NODE_ROWS, (NODES - 1) * PAIR_ROWS, sem)

    def wait_slots(flat, ref, sem):
        either(flat, ref, (LOCALS - 1) * CAP, REMOTE * CAP, sem)

    def flat_node_send(k):
        zs[k, 0:ROWS, :] = mm(choose[0], tok[:, columns(k)]).astype(BF16)
        to_nodes(zs.at[k], passed.at[k], NODE_ROWS, sem_z.at[0, k], sem_z.at[1, k])
        passed[k, rows_at(node, NODE_ROWS), :] = zs[k, rows_at(node, NODE_ROWS), :]

    def put_pair(slot, side, value):
        for n in range(NODES):
            at = n * PAIR_ROWS + side * NODE_ROWS
            zs[slot, at : at + NODE_ROWS, :] = value[n * NODE_ROWS : (n + 1) * NODE_ROWS, :]

    def get_pair(ref, k, side):
        starts = [n * PAIR_ROWS + side * NODE_ROWS for n in range(NODES)]
        return jnp.concatenate([ref[k, at : at + NODE_ROWS, :] for at in starts], axis=0)

    def node_send(k):
        t = lax.rem(k, TYPES)
        slot = lax.rem(k, ZS_SLOTS)

        @pl.when(k < FLAT_FIRST + TYPES)
        def _():
            wait_for(named_in.at[t], sem_named.at[1, t])
            route(1 + t, named_in[t])

        @pl.when(k >= ZS_SLOTS)
        def _():
            old = k - ZS_SLOTS
            wait_node_rows(old < FLAT_FIRST, zs.at[slot], sem_z.at[0, old])

        put_pair(slot, 0, mm(choose[0], tok[:, columns(k)]).astype(BF16))
        wait_for(shared.at[k], sem_shared.at[1, k])
        put_pair(slot, 1, mm(choose[1 + t], shared[k]).astype(BF16))
        to_nodes(zs.at[slot], passed.at[k], PAIR_ROWS, sem_z.at[0, k], sem_z.at[1, k])
        passed[k, rows_at(node, PAIR_ROWS), :] = zs[slot, rows_at(node, PAIR_ROWS), :]

    def count_rows(who):
        routed = ones_where(gates[who].astype(F32) > 0.0)
        before = ones_where(iota((ROWS, ROWS), 1) <= iota((ROWS, ROWS), 0)).astype(BF16)
        count = mm(before, routed.astype(BF16))
        counts[who] = jnp.where(routed > 0.0, jnp.minimum(count, 255.0), 0.0).astype(BF16)

    def expert_lane(slot, t):
        along_x, way = kind(t)
        i = lax.div(slot, CAP)
        a, b = i >> 2, i & 3
        on_y = y + a * (paired(y, 1 - way) - y)
        on_x = x + a * (paired(x, 1 - way) - x)
        lane_y = on_y * SIDE + ((x + b) & 3)
        lane_x = ((y + b) & 3) * SIDE + on_x
        return node * LOCALS + (1 - along_x) * lane_y + along_x * lane_x

    def build_pick(t):
        @pl.loop(0, 2 * HALF // BUILD)
        def _(j):
            side = j // (HALF // BUILD)
            i = lax.rem(j, HALF // BUILD)
            who = side * (1 + t)
            slot = iota((BUILD, TOK), 0) + i * BUILD
            spread = ones_where(iota((BUILD, TOK), 1) == expert_lane(slot, t)).astype(BF16)
            count_at = mm_nt(spread, counts[who])
            wanted = (lax.rem(iota((BUILD, ROWS), 0) + i * BUILD, CAP) + 1).astype(F32)
            moves[t, side, rows_at(i, BUILD), :] = ones_where(count_at == wanted).astype(BF16)

    def build_combine(t):
        @pl.loop(0, 2 * HALF // BUILD)
        def _(j):
            side = j // (HALF // BUILD)
            i = lax.rem(j, HALF // BUILD)
            who = side * (1 + t)
            slot = iota((TOK, BUILD), 1) + i * BUILD
            spread = ones_where(iota((TOK, BUILD), 0) == expert_lane(slot, t)).astype(BF16)
            count_at = mm(counts[who], spread)
            gate_at = mm(gates[who], spread)
            wanted = (lax.rem(iota((8, BUILD), 1) + i * BUILD, CAP)[0:1, :] + 1).astype(F32)
            weight = jnp.where(count_at == wanted, gate_at, 0.0).astype(BF16)
            for q in range(ROWS // BUILD):
                moves[t, side, rows_at(i, BUILD), q * BUILD : (q + 1) * BUILD] = weight[
                    q * BUILD : (q + 1) * BUILD, :
                ]

    def build_flat_pick():
        @pl.loop(0, SLOTS // BUILD)
        def _(i):
            slot = iota((BUILD, TOK), 0) + i * BUILD
            lane = node * LOCALS + lax.div(slot, CAP)
            spread = ones_where(iota((BUILD, TOK), 1) == lane).astype(BF16)
            count_at = mm_nt(spread, counts[0])
            wanted = (lax.rem(iota((BUILD, ROWS), 0) + i * BUILD, CAP) + 1).astype(F32)
            hidden[rows_at(i, BUILD), 0:ROWS] = ones_where(count_at == wanted).astype(BF16)

    def build_flat_combine():
        @pl.loop(0, SLOTS // BUILD)
        def _(i):
            slot = iota((TOK, BUILD), 1) + i * BUILD
            lane = node * LOCALS + lax.div(slot, CAP)
            spread = ones_where(iota((TOK, BUILD), 0) == lane).astype(BF16)
            count_at = mm(counts[0], spread)
            gate_at = mm(gates[0], spread)
            wanted = (lax.rem(iota((8, BUILD), 1) + i * BUILD, CAP)[0:1, :] + 1).astype(F32)
            weight = jnp.where(count_at == wanted, gate_at, 0.0)
            for q in range(ROWS // BUILD):
                acc_up[rows_at(i, BUILD), q * BUILD : (q + 1) * BUILD] = weight[
                    q * BUILD : (q + 1) * BUILD, :
                ]

    @pl.loop(0, FLAT_FIRST)
    def _(k):
        flat_node_send(k)

    @pl.loop(0, TYPES)
    def _(t):
        there = (node, partner_at(t))
        send(named, named_in.at[t], sem_named.at[0, t], sem_named.at[1, t], there)

    @pl.loop(FLAT_FIRST, chunks)
    def _(k):
        there = (node, partner_at(k))
        send(
            tok.at[:, columns(k)], shared.at[k], sem_shared.at[0, k], sem_shared.at[1, k], there
        )

    gates[0, rows_at(node, NODE_ROWS), :] = gate_out[rows_at(node, NODE_ROWS), :]

    node_send(FLAT_FIRST)
    wait_for(gates.at[0, pl.ds(0, (NODES - 1) * NODE_ROWS)], sem_misc.at[1])

    @pl.loop(0, TYPES)
    def _(t):
        there = (node, partner_at(t))
        send(gates.at[0], gates.at[1 + t], sem_gates.at[0, t], sem_gates.at[1, t], there)

    count_rows(0)
    build_flat_pick()

    @pl.loop(FLAT_FIRST + 1, AHEAD)
    def _(k):
        node_send(k)

    lat_rows = LOCALS * NODES * 2

    def latent_first():
        width = latent_cache.shape[0]
        lat_pad[0:width, :] = lat_t[...]
        lat_pad[width:, :] = ones_where(iota((LAT_PAD - width, TOK), 0) == 0).astype(BF16)
        row = iota((lat_rows, TOK), 0)
        owner_of_row = (((row & 15) >> 1) << 4) + (row >> 4)
        owned = ones_where(owner[...] == owner_of_row)
        upto = ones_where(iota((TOK, TOK), 0) <= iota((TOK, TOK), 1)).astype(BF16)
        rank = mm(owned.astype(BF16), upto)
        lat_pick = jnp.where(rank == ((row & 1) + 1).astype(F32), owned, 0.0).astype(BF16)
        lat_s1[...] = mm_nt(lat_pick, lat_pad[...]).astype(BF16)
        to_locals(lat_s1, lat_r1, 16, sem_misc.at[2], sem_misc.at[3])
        lat_r1[rows_at(local, 16), :] = lat_s1[rows_at(local, 16), :]

    def latent_second():
        wait_for(lat_r1.at[pl.ds(0, lat_rows - 16)], sem_misc.at[3])
        row = iota((lat_rows, lat_rows), 0)
        source = (((row & 31) >> 1) << 4) + ((row >> 5) << 1) + (row & 1)
        turn = ones_where(iota((lat_rows, lat_rows), 1) == source).astype(BF16)
        lat_s2[...] = mm(turn, lat_r1[...]).astype(BF16)
        to_nodes(lat_s2, lat_r2, 32, sem_misc.at[4], sem_misc.at[5])
        lat_r2[rows_at(node, 32), :] = lat_s2[rows_at(node, 32), :]

    def latent_third():
        wait_for(lat_r2.at[pl.ds(0, lat_rows - 32)], sem_misc.at[5])
        arrived = lat_r2[...]
        mark = ones_where(iota((8, LAT_PAD), 1) == latent_cache.shape[0]).astype(BF16)
        live = mm_nt(mark, arrived)
        upto = ones_where(iota((lat_rows, lat_rows), 0) <= iota((lat_rows, lat_rows), 1))
        place = mm(live.astype(BF16), upto.astype(BF16))
        wanted = (iota((TOK, lat_rows), 0) + 1).astype(F32)
        settle = jnp.where(place[0:1, :] == wanted, live[0:1, :], 0.0).astype(BF16)
        settled = jnp.transpose(mm(settle, arrived))
        latent_cache[...] = settled[0 : latent_cache.shape[0], :].astype(BF16)

    def wait_group(k, cy):
        py, _ = partner_of(y, x, k)
        pairs = (k >= FLAT_FIRST) & (cy == py)
        missing = (cy == y).astype(jnp.int32) + pairs.astype(jnp.int32)
        for skipped in range(3):

            @pl.when(missing == skipped)
            def _():
                wait_for(rx.at[k, pl.ds(0, GROUP - skipped * CAP)], sem_rx.at[k, cy])

    def expert_in(k):
        for copy in weights_in(k):
            copy.wait()
        slot = lax.rem(k, 2)

        @pl.loop(0, SIDE)
        def _(g):
            cy = lax.rem(y + g, SIDE)
            wait_group(k, cy)
            rows = rows_at(cy, GROUP)
            part = rx[k, rows, :]

            @pl.when(k == 0)
            def _():
                acc_gate[rows, :] = mm(part, wg_buf[slot])
                acc_up[rows, :] = mm(part, wu_buf[slot])

            @pl.when(k > 0)
            def _():
                acc_gate[rows, :] += mm(part, wg_buf[slot])
                acc_up[rows, :] += mm(part, wu_buf[slot])

        @pl.when(k + 2 < chunks)
        def _():
            for copy in weights_in(k + 2):
                copy.start()

    def paired_rows(k):
        t = lax.rem(k, TYPES)
        slot = lax.rem(k, TX_SLOTS)

        @pl.when(k < FLAT_FIRST + TYPES)
        def _():
            wait_for(gates.at[1 + t], sem_gates.at[1, t])
            count_rows(1 + t)
            build_pick(t)

        wait_for(passed.at[k, pl.ds(0, (NODES - 1) * PAIR_ROWS)], sem_z.at[1, k])

        @pl.when(k >= TX_SLOTS)
        def _():
            old = k - TX_SLOTS
            wait_slots(old < FLAT_FIRST, tx.at[slot], sem_tx.at[old])

        for side in range(2):
            arrived = get_pair(passed, k, side)
            rows = pl.ds(side * HALF, HALF)
            tx[slot, rows, :] = mm(moves[t, side], arrived).astype(BF16)

        py, px = partner_of(y, x, k)

        @pl.loop(0, REMOTE)
        def _(m):
            side = m // (COVER - 1)
            i = 1 + lax.rem(m * STRIDE, COVER - 1)
            ey, ex = cover(k, i // SIDE, lax.rem(i, SIDE))
            cy = y + side * (py - y)
            cx = x + side * (px - x)
            send(
                tx.at[slot, rows_at(side * COVER + i, CAP)],
                rx.at[k, rows_at(cy * SIDE + cx, CAP)],
                sem_tx.at[k],
                sem_rx.at[k, cy],
                (node, ey * SIDE + ex),
            )

        rx[k, rows_at(local, CAP), :] = tx[slot, 0:CAP, :]
        rx[k, rows_at(py * SIDE + px, CAP), :] = tx[slot, HALF : HALF + CAP, :]

    def flat_rows(k):
        wait_for(passed.at[k, pl.ds(0, (NODES - 1) * NODE_ROWS)], sem_z.at[1, k])
        tx[k] = mm(hidden[:, 0:ROWS], passed[k, 0:ROWS, :]).astype(BF16)

        @pl.loop(1, LOCALS)
        def _(d):
            peer = local_peer(lax.rem(d * STRIDE, LOCALS))
            send(
                tx.at[k, rows_at(peer, CAP)],
                rx.at[k, rows_at(local, CAP)],
                sem_tx.at[k],
                sem_rx.at[k, y],
                (node, peer),
            )

        rx[k, rows_at(local, CAP), :] = tx[k, rows_at(local, CAP), :]

    @pl.loop(0, chunks - 1 + EXPERT_LAG)
    def _(k):
        @pl.when(k < FLAT_FIRST)
        def _():
            flat_rows(k)

        @pl.when((k >= FLAT_FIRST) & (k < chunks))
        def _():
            paired_rows(k)

        @pl.when(k + AHEAD < chunks)
        def _():
            node_send(k + AHEAD)

        @pl.when(k == 4)
        def _():
            latent_first()

        @pl.when(k == 8)
        def _():
            latent_second()

        @pl.when(k >= EXPERT_LAG)
        def _():
            expert_in(k - EXPERT_LAG)

    def send_back(k, a, b, side):
        fy, fx = cover(k, a, b)
        py, px = partner_of(fy, fx, k)
        cy = fy + side * (py - fy)
        cx = fx + side * (px - fx)
        i = a * SIDE + lax.rem(SIDE - b, SIDE)
        send(
            rx.at[k, rows_at(cy * SIDE + cx, CAP)],
            passed.at[k, rows_at(side * COVER + i, CAP)],
            sem_ret.at[0, k],
            sem_ret.at[1, k],
            (node, fy * SIDE + fx),
        )

    def keep_back(k):
        passed[k, 0:CAP, :] = rx[k, rows_at(local, CAP), :]
        passed[k, HALF : HALF + CAP, :] = rx[k, rows_at(partner_at(k), CAP), :]

    last = chunks - 1
    for copy in weights_in(last):
        copy.wait()
    down_in(0).wait()

    @pl.loop(0, SIDE)
    def _(g):
        a, side = lax.rem(g, 2), g // 2
        fy, fx = cover(0, a, 0)
        py, _ = partner_of(fy, fx, 0)
        there = fy + side * (py - fy)
        wait_group(last, there)
        rows = rows_at(there, GROUP)
        part = rx[last, rows, :]
        gate_act = acc_gate[rows, :] + mm(part, wg_buf[last % 2])
        up_act = acc_up[rows, :] + mm(part, wu_buf[last % 2])
        hidden[rows, :] = (gate_act / (1.0 + jnp.exp(-gate_act)) * up_act).astype(BF16)
        rx[0, rows, :] = mm(hidden[rows, :], wd_buf[0]).astype(BF16)

        @pl.loop(0, SIDE)
        def _(b):
            @pl.when(a + b > 0)
            def _():
                send_back(0, a, b, side)

    keep_back(0)
    down_in(2).start()

    @pl.loop(chunks - ZS_SLOTS, chunks)
    def _(k):
        wait_for(zs.at[0, pl.ds(0, (NODES - 1) * PAIR_ROWS)], sem_z.at[0, k])

    @pl.loop(chunks - TX_SLOTS, chunks)
    def _(k):
        wait_for(tx.at[0, pl.ds(0, REMOTE * CAP)], sem_tx.at[k])

    parts = [pl.ds(i * BUILD, BUILD) for i in range(HALF // BUILD)]

    def node_part(k):
        t = lax.rem(k, TYPES)
        slot = lax.rem(k, ZS_SLOTS)

        @pl.when(k < TYPES)
        def _():
            build_combine(t)

        wait_for(passed.at[k, pl.ds(0, REMOTE * CAP)], sem_ret.at[1, k])

        @pl.when(k >= ZS_SLOTS)
        def _():
            old = k - ZS_SLOTS
            wait_node_rows(old >= flat_back, zs.at[slot], sem_back.at[0, old])

        for side in range(2):
            weight = jnp.concatenate(
                [
                    jnp.concatenate(
                        [moves[t, side, part, pl.ds(q * BUILD, BUILD)] for part in parts], axis=1
                    )
                    for q in range(ROWS // BUILD)
                ],
                axis=0,
            )
            total = mm(weight, passed[k, side * HALF : (side + 1) * HALF, :])
            put_pair(slot, side, total.astype(BF16))

        to_nodes(zs.at[slot], back.at[k], PAIR_ROWS, sem_back.at[0, k], sem_back.at[1, k])
        back[k, rows_at(node, PAIR_ROWS), :] = zs[slot, rows_at(node, PAIR_ROWS), :]

    flat_parts = [pl.ds(i * BUILD, BUILD) for i in range(SLOTS // BUILD)]

    def flat_part(k):
        slot = lax.rem(k, ZS_SLOTS)
        wait_for(passed.at[k, pl.ds(0, (LOCALS - 1) * CAP)], sem_ret.at[1, k])
        old = k - ZS_SLOTS
        wait_node_rows(old >= flat_back, zs.at[slot], sem_back.at[0, old])
        for q in range(ROWS // BUILD):
            weight = jnp.concatenate(
                [acc_up[part, pl.ds(q * BUILD, BUILD)] for part in flat_parts], axis=1
            ).astype(BF16)
            zs[slot, q * BUILD : (q + 1) * BUILD, :] = mm(weight, passed[k]).astype(BF16)
        to_nodes(zs.at[slot], back.at[k], NODE_ROWS, sem_back.at[0, k], sem_back.at[1, k])
        back[k, rows_at(node, NODE_ROWS), :] = zs[slot, rows_at(node, NODE_ROWS), :]

    def flat_finish(k):
        wait_for(back.at[k, pl.ds(0, (NODES - 1) * NODE_ROWS)], sem_back.at[1, k])
        moe[:, columns(k)] = mm(choose_t[0], back[k, 0:ROWS, :]).astype(BF16)

    def to_partner(k):
        t = lax.rem(k, TYPES)

        @pl.when(k < TYPES)
        def _():
            choose_t[1 + t] = jnp.transpose(choose[1 + t].astype(F32)).astype(BF16)

        wait_for(back.at[k, pl.ds(0, (NODES - 1) * PAIR_ROWS)], sem_back.at[1, k])
        shared[k] = mm(choose_t[1 + t], get_pair(back, k, 1)).astype(BF16)
        there = (node, partner_at(k))
        send(shared.at[k], shared_back.at[k], sem_home.at[0, k], sem_home.at[1, k], there)

    def finish(k):
        own = mm(choose_t[0], get_pair(back, k, 0))
        wait_for(shared_back.at[k], sem_home.at[1, k])
        moe[:, columns(k)] = (own + shared_back[k].astype(F32)).astype(BF16)

    choose_t[0] = jnp.transpose(choose[0].astype(F32)).astype(BF16)

    @pl.loop(1, chunks + END_LAG)
    def _(k):
        @pl.when(k < chunks)
        def _():
            slot = lax.rem(k, 2)
            down_in(k).wait()

            @pl.loop(0, SIDE)
            def _(i):
                rows = rows_at(i, GROUP)
                rx[k, rows, :] = mm(hidden[rows, :], wd_buf[slot]).astype(BF16)

            @pl.when(k < flat_back)
            def _():
                @pl.loop(0, REMOTE)
                def _(m):
                    j = 1 + lax.rem(m * STRIDE, COVER - 1)
                    send_back(k, j // SIDE, lax.rem(j, SIDE), m // (COVER - 1))

                keep_back(k)

            @pl.when(k >= flat_back)
            def _():
                to_locals(rx.at[k], passed.at[k], CAP, sem_ret.at[0, k], sem_ret.at[1, k])
                passed[k, rows_at(local, CAP), :] = rx[k, rows_at(local, CAP), :]

            @pl.when(k + 2 < chunks)
            def _():
                down_in(k + 2).start()

        @pl.when((k >= PART_LAG) & (k < flat_back + PART_LAG))
        def _():
            node_part(k - PART_LAG)

        @pl.when((k >= flat_back + PART_LAG) & (k < chunks + PART_LAG))
        def _():
            flat_part(k - PART_LAG)

        @pl.when(k == 10)
        def _():
            build_flat_combine()

        @pl.when(k == 9)
        def _():
            latent_third()

        @pl.when((k >= HOME_LAG) & (k < flat_back + HOME_LAG))
        def _():
            to_partner(k - HOME_LAG)

        @pl.when((k >= END_LAG) & (k < flat_back + END_LAG))
        def _():
            finish(k - END_LAG)

        @pl.when(k >= flat_back + END_LAG)
        def _():
            flat_finish(k - END_LAG)

    @pl.loop(FLAT_FIRST, chunks)
    def _(k):
        wait_for(shared.at[k], sem_shared.at[0, k])

    @pl.loop(0, chunks)
    def _(k):
        wait_slots(k >= flat_back, rx.at[k], sem_ret.at[0, k])

    @pl.loop(0, flat_back)
    def _(k):
        wait_for(shared.at[k], sem_home.at[0, k])

    @pl.loop(chunks - ZS_SLOTS, chunks)
    def _(k):
        wait_node_rows(k >= flat_back, zs.at[0], sem_back.at[0, k])

    @pl.loop(0, TYPES)
    def _(t):
        wait_for(named, sem_named.at[0, t])
        wait_for(gates.at[0], sem_gates.at[0, t])

    wait_for(gate_out.at[pl.ds(0, (NODES - 1) * NODE_ROWS)], sem_misc.at[0])
    wait_for(lat_s1.at[pl.ds(0, lat_rows - 16)], sem_misc.at[2])
    wait_for(lat_s2.at[pl.ds(0, lat_rows - 32)], sem_misc.at[4])


def per_device(tokens, ids, weights, wg, wu, wd, latent_rows, latent_owner):
    count, width = tokens.shape
    lat_width = latent_rows.shape[1]
    hidden_width = wg.shape[2]
    chunks = width // WIDTH
    vmem = pl.BlockSpec(memory_space=pltpu.VMEM)
    hbm = pl.BlockSpec(memory_space=pl.ANY)
    lat_all = LOCALS * NODES * 2
    dma = pltpu.SemaphoreType.DMA
    moe, cache_t = pl.pallas_call(
        functools.partial(kernel, chunks),
        out_shape=(
            jax.ShapeDtypeStruct((count, width), BF16),
            jax.ShapeDtypeStruct((lat_width, count), BF16),
        ),
        in_specs=[vmem] * 5 + [hbm] * 3,
        out_specs=(vmem, vmem),
        scratch_shapes=[
            pltpu.VMEM((2 * ids.shape[1], TOK), F32),
            pltpu.VMEM((TYPES, 2 * ids.shape[1], TOK), F32),
            pltpu.VMEM((1 + TYPES, ROWS, TOK), BF16),
            pltpu.VMEM((1 + TYPES, TOK, ROWS), BF16),
            pltpu.VMEM((1 + TYPES, ROWS, TOK), BF16),
            pltpu.VMEM((1 + TYPES, ROWS, TOK), BF16),
            pltpu.VMEM((ROWS, TOK), BF16),
            pltpu.VMEM((TYPES, 2, HALF, ROWS), BF16),
            pltpu.VMEM((chunks, TOK, WIDTH), BF16),
            pltpu.VMEM((chunks, TOK, WIDTH), BF16),
            pltpu.VMEM((ZS_SLOTS, NODES * PAIR_ROWS, WIDTH), BF16),
            pltpu.VMEM((chunks, SLOTS, WIDTH), BF16),
            pltpu.VMEM((TX_SLOTS, SLOTS, WIDTH), BF16),
            pltpu.VMEM((chunks, SLOTS, WIDTH), BF16),
            pltpu.VMEM((chunks, NODES * PAIR_ROWS, WIDTH), BF16),
            pltpu.VMEM((SLOTS, hidden_width), F32),
            pltpu.VMEM((SLOTS, hidden_width), F32),
            pltpu.VMEM((SLOTS, hidden_width), BF16),
            pltpu.VMEM((2, WIDTH, hidden_width), BF16),
            pltpu.VMEM((2, WIDTH, hidden_width), BF16),
            pltpu.VMEM((2, hidden_width, WIDTH), BF16),
            pltpu.VMEM((LAT_PAD, count), BF16),
            pltpu.VMEM((lat_all, LAT_PAD), BF16),
            pltpu.VMEM((lat_all, LAT_PAD), BF16),
            pltpu.VMEM((lat_all, LAT_PAD), BF16),
            pltpu.VMEM((lat_all, LAT_PAD), BF16),
            dma((3, 2)),
            dma((2, TYPES)),
            dma((2, TYPES)),
            dma((2, chunks)),
            dma((2, chunks)),
            dma((2, chunks)),
            dma((chunks,)),
            dma((chunks, SIDE)),
            dma((2, chunks)),
            dma((2, chunks)),
            dma((6,)),
        ],
        compiler_params=pltpu.CompilerParams(
            collective_id=0, has_side_effects=True, vmem_limit_bytes=62 * 2**20
        ),
        cost_estimate=pl.CostEstimate(
            flops=6 * SLOTS * width * hidden_width,
            bytes_accessed=6 * width * hidden_width,
            transcendentals=SLOTS * hidden_width,
        ),
        name="moe_exchange",
    )(
        tokens,
        jnp.transpose(ids),
        jnp.transpose(weights),
        jnp.transpose(latent_rows),
        latent_owner.reshape(1, count),
        wg,
        wu,
        wd,
    )
    return moe, jnp.transpose(cache_t)


def solution(mesh):
    rows = P(("node", "local"), None)
    experts = P(("node", "local"), None, None)
    return jax.shard_map(
        per_device,
        mesh=mesh,
        in_specs=(rows, rows, rows, experts, experts, experts, rows, P(("node", "local"))),
        out_specs=(rows, rows),
        check_vma=False,
    )
```

```python
import functools

import jax
import jax.numpy as jnp
from jax import lax
from jax.experimental import pallas as pl
from jax.experimental.pallas import tpu as pltpu
from jax.sharding import PartitionSpec as P

MESH = pl.DeviceIdType.MESH
BF16 = jnp.bfloat16
F32 = jnp.float32

NODES = 8
LOCALS = 16
SIDE = 4
TYPES = 4
COVER = 8
CAP = 80
NODE_ROWS = 64
PAIR_ROWS = 2 * NODE_ROWS
TOK = 128
ROWS = NODES * NODE_ROWS
SLOTS = LOCALS * CAP
HALF = COVER * CAP
GROUP = SIDE * CAP
REMOTE = 2 * (COVER - 1)
WIDTH = 256
TX_SLOTS = 6
ZS_SLOTS = 4
AHEAD = 3
EXPERT_LAG = 4
PART_LAG = 5
HOME_LAG = 7
END_LAG = 8
FLAT_FIRST = 2
FLAT_LAST = 3
STRIDE = 3
BUILD = 128
LAT_PAD = 640


def iota(shape, dim):
    return lax.broadcasted_iota(jnp.int32, shape, dim)


def mm(a, b):
    return jnp.dot(a, b, preferred_element_type=F32)


def mm_nt(a, b):
    return lax.dot_general(a, b, (((1,), (1,)), ((), ())), preferred_element_type=F32)


def ones_where(mask):
    return jnp.where(mask, 1.0, 0.0)


def wait_for(ref, sem):
    pltpu.make_async_copy(ref, ref, sem).wait()


def rows_at(index, size):
    return pl.ds(pl.multiple_of(index * size, size), size)


def kernel(
    chunks,
    tok,
    ids_t,
    weights_t,
    lat_t,
    owner,
    wg,
    wu,
    wd,
    moe,
    latent_cache,
    named,
    named_in,
    choose,
    choose_t,
    gates,
    counts,
    gate_out,
    moves,
    shared,
    shared_back,
    zs,
    passed,
    tx,
    rx,
    back,
    acc_gate,
    acc_up,
    hidden,
    wg_buf,
    wu_buf,
    wd_buf,
    lat_pad,
    lat_s1,
    lat_r1,
    lat_s2,
    lat_r2,
    sem_w,
    sem_named,
    sem_gates,
    sem_shared,
    sem_home,
    sem_z,
    sem_tx,
    sem_rx,
    sem_ret,
    sem_back,
    sem_misc,
):
    node = lax.axis_index("node")
    local = lax.axis_index("local")
    z, core = node // 2, lax.rem(node, 2)
    y, x = local // SIDE, lax.rem(local, SIDE)

    def node_peer(d):
        dz, dc = d // 2, lax.rem(d, 2)
        return lax.rem(z + dz, SIDE) * 2 + lax.rem(core + dc, 2)

    def local_peer(d):
        dy, dx = d // SIDE, lax.rem(d, SIDE)
        return lax.rem(y + dy, SIDE) * SIDE + lax.rem(x + dx, SIDE)

    def paired(v, way):
        return (1 - way) * (v + 1 - 2 * lax.rem(v, 2)) + way * (SIDE - 1 - v)

    def kind(k):
        t = lax.rem(k, TYPES)
        return t // 2, lax.rem(t, 2)

    def partner_of(py, px, t):
        along_x, way = kind(t)
        return (
            py + (1 - along_x) * (paired(py, way) - py),
            px + along_x * (paired(px, way) - px),
        )

    def partner_at(t):
        py, px = partner_of(y, x, t)
        return py * SIDE + px

    def cover(t, a, b):
        along_x, way = kind(t)
        cy = (1 - along_x) * (y + a * (paired(y, 1 - way) - y)) + along_x * lax.rem(y + b, SIDE)
        cx = along_x * (x + a * (paired(x, 1 - way) - x)) + (1 - along_x) * lax.rem(x + b, SIDE)
        return cy, cx

    def send(src, dst, send_sem, recv_sem, device):
        pltpu.make_async_remote_copy(
            src_ref=src,
            dst_ref=dst,
            send_sem=send_sem,
            recv_sem=recv_sem,
            device_id=device,
            device_id_type=MESH,
        ).start()

    def to_nodes(src, dst, size, send_sem, recv_sem):
        @pl.loop(1, NODES)
        def _(d):
            peer = node_peer(d)
            send(
                src.at[rows_at(peer, size)],
                dst.at[rows_at(node, size)],
                send_sem,
                recv_sem,
                (peer, local),
            )

    def to_locals(src, dst, size, send_sem, recv_sem):
        @pl.loop(1, LOCALS)
        def _(d):
            peer = local_peer(lax.rem(d * STRIDE, LOCALS))
            send(
                src.at[rows_at(peer, size)],
                dst.at[rows_at(local, size)],
                send_sem,
                recv_sem,
                (node, peer),
            )

    def columns(k):
        return pl.ds(pl.multiple_of(k * WIDTH, WIDTH), WIDTH)

    def weights_in(k):
        slot = lax.rem(k, 2)
        return (
            pltpu.make_async_copy(wg.at[0, columns(k)], wg_buf.at[slot], sem_w.at[0, slot]),
            pltpu.make_async_copy(wu.at[0, columns(k)], wu_buf.at[slot], sem_w.at[1, slot]),
        )

    def down_in(k):
        slot = lax.rem(k, 2)
        return pltpu.make_async_copy(wd.at[0, :, columns(k)], wd_buf.at[slot], sem_w.at[2, slot])

    barrier = pltpu.get_barrier_semaphore()

    @pl.loop(1, LOCALS)
    def _(d):
        pl.semaphore_signal(barrier, inc=1, device_id=(node, local_peer(d)), device_id_type=MESH)

    @pl.loop(1, NODES)
    def _(d):
        pl.semaphore_signal(barrier, inc=1, device_id=(node_peer(d), local), device_id_type=MESH)

    for copy in weights_in(0) + weights_in(1):
        copy.start()
    down_in(0).start()
    down_in(1).start()
    named[0 : ids_t.shape[0], :] = ids_t[...].astype(F32)
    named[ids_t.shape[0] :, :] = weights_t[...].astype(F32)

    def route(who, names):
        gates_t = jnp.zeros((TOK, TOK), F32)
        expert_row = iota((TOK, TOK), 0).astype(F32)
        top = ids_t.shape[0]
        for k in range(top):
            hit = names[k : k + 1, :] == expert_row
            gates_t += jnp.where(hit, names[top + k : top + k + 1, :], 0.0)
        hit_t = ones_where(gates_t > 0.0).astype(BF16)
        upto = ones_where(iota((TOK, TOK), 0) <= iota((TOK, TOK), 1)).astype(BF16)
        of_node = ones_where((iota((ROWS, TOK), 0) >> 6) == (iota((ROWS, TOK), 1) >> 4))
        reached = ones_where(mm(of_node.astype(BF16), hit_t) > 0.0)
        rank = mm(reached.astype(BF16), upto)
        slot_in_node = ((iota((ROWS, TOK), 0) & (NODE_ROWS - 1)) + 1).astype(F32)
        choose[who] = jnp.where(rank == slot_in_node, reached, 0.0).astype(BF16)
        return gates_t

    own_gates = jnp.transpose(route(0, named[...])).astype(BF16)
    gate_out[...] = mm(choose[0], own_gates).astype(BF16)

    pl.semaphore_wait(barrier, NODES - 1 + LOCALS - 1)

    to_nodes(gate_out, gates.at[0], NODE_ROWS, sem_misc.at[0], sem_misc.at[1])

    flat_back = chunks - FLAT_LAST

    def either(flat, ref, flat_rows, rows, sem):
        @pl.when(flat)
        def _():
            wait_for(ref.at[pl.ds(0, flat_rows)], sem)

        @pl.when(jnp.logical_not(flat))
        def _():
            wait_for(ref.at[pl.ds(0, rows)], sem)

    def wait_node_rows(flat, ref, sem):
        either(flat, ref, (NODES - 1) * NODE_ROWS, (NODES - 1) * PAIR_ROWS, sem)

    def wait_slots(flat, ref, sem):
        either(flat, ref, (LOCALS - 1) * CAP, REMOTE * CAP, sem)

    def flat_node_send(k):
        zs[k, 0:ROWS, :] = mm(choose[0], tok[:, columns(k)]).astype(BF16)
        to_nodes(zs.at[k], passed.at[k], NODE_ROWS, sem_z.at[0, k], sem_z.at[1, k])
        passed[k, rows_at(node, NODE_ROWS), :] = zs[k, rows_at(node, NODE_ROWS), :]

    def put_pair(slot, side, value):
        for n in range(NODES):
            at = n * PAIR_ROWS + side * NODE_ROWS
            zs[slot, at : at + NODE_ROWS, :] = value[n * NODE_ROWS : (n + 1) * NODE_ROWS, :]

    def get_pair(ref, k, side):
        starts = [n * PAIR_ROWS + side * NODE_ROWS for n in range(NODES)]
        return jnp.concatenate([ref[k, at : at + NODE_ROWS, :] for at in starts], axis=0)

    def node_send(k):
        t = lax.rem(k, TYPES)
        slot = lax.rem(k, ZS_SLOTS)

        @pl.when(k < FLAT_FIRST + TYPES)
        def _():
            wait_for(named_in.at[t], sem_named.at[1, t])
            route(1 + t, named_in[t])

        @pl.when(k >= ZS_SLOTS)
        def _():
            old = k - ZS_SLOTS
            wait_node_rows(old < FLAT_FIRST, zs.at[slot], sem_z.at[0, old])

        put_pair(slot, 0, mm(choose[0], tok[:, columns(k)]).astype(BF16))
        wait_for(shared.at[k], sem_shared.at[1, k])
        put_pair(slot, 1, mm(choose[1 + t], shared[k]).astype(BF16))
        to_nodes(zs.at[slot], passed.at[k], PAIR_ROWS, sem_z.at[0, k], sem_z.at[1, k])
        passed[k, rows_at(node, PAIR_ROWS), :] = zs[slot, rows_at(node, PAIR_ROWS), :]

    def count_rows(who):
        routed = ones_where(gates[who].astype(F32) > 0.0)
        before = ones_where(iota((ROWS, ROWS), 1) <= iota((ROWS, ROWS), 0)).astype(BF16)
        count = mm(before, routed.astype(BF16))
        counts[who] = jnp.where(routed > 0.0, jnp.minimum(count, 255.0), 0.0).astype(BF16)

    def expert_lane(slot, t):
        along_x, way = kind(t)
        i = lax.div(slot, CAP)
        a, b = i >> 2, i & 3
        on_y = y + a * (paired(y, 1 - way) - y)
        on_x = x + a * (paired(x, 1 - way) - x)
        lane_y = on_y * SIDE + ((x + b) & 3)
        lane_x = ((y + b) & 3) * SIDE + on_x
        return node * LOCALS + (1 - along_x) * lane_y + along_x * lane_x

    def build_pick(t):
        @pl.loop(0, 2 * HALF // BUILD)
        def _(j):
            side = j // (HALF // BUILD)
            i = lax.rem(j, HALF // BUILD)
            who = side * (1 + t)
            slot = iota((BUILD, TOK), 0) + i * BUILD
            spread = ones_where(iota((BUILD, TOK), 1) == expert_lane(slot, t)).astype(BF16)
            count_at = mm_nt(spread, counts[who])
            wanted = (lax.rem(iota((BUILD, ROWS), 0) + i * BUILD, CAP) + 1).astype(F32)
            moves[t, side, rows_at(i, BUILD), :] = ones_where(count_at == wanted).astype(BF16)

    def build_combine(t):
        @pl.loop(0, 2 * HALF // BUILD)
        def _(j):
            side = j // (HALF // BUILD)
            i = lax.rem(j, HALF // BUILD)
            who = side * (1 + t)
            slot = iota((TOK, BUILD), 1) + i * BUILD
            spread = ones_where(iota((TOK, BUILD), 0) == expert_lane(slot, t)).astype(BF16)
            count_at = mm(counts[who], spread)
            gate_at = mm(gates[who], spread)
            wanted = (lax.rem(iota((8, BUILD), 1) + i * BUILD, CAP)[0:1, :] + 1).astype(F32)
            weight = jnp.where(count_at == wanted, gate_at, 0.0).astype(BF16)
            for q in range(ROWS // BUILD):
                moves[t, side, rows_at(i, BUILD), q * BUILD : (q + 1) * BUILD] = weight[
                    q * BUILD : (q + 1) * BUILD, :
                ]

    def build_flat_pick():
        @pl.loop(0, SLOTS // BUILD)
        def _(i):
            slot = iota((BUILD, TOK), 0) + i * BUILD
            lane = node * LOCALS + lax.div(slot, CAP)
            spread = ones_where(iota((BUILD, TOK), 1) == lane).astype(BF16)
            count_at = mm_nt(spread, counts[0])
            wanted = (lax.rem(iota((BUILD, ROWS), 0) + i * BUILD, CAP) + 1).astype(F32)
            hidden[rows_at(i, BUILD), 0:ROWS] = ones_where(count_at == wanted).astype(BF16)

    def build_flat_combine():
        @pl.loop(0, SLOTS // BUILD)
        def _(i):
            slot = iota((TOK, BUILD), 1) + i * BUILD
            lane = node * LOCALS + lax.div(slot, CAP)
            spread = ones_where(iota((TOK, BUILD), 0) == lane).astype(BF16)
            count_at = mm(counts[0], spread)
            gate_at = mm(gates[0], spread)
            wanted = (lax.rem(iota((8, BUILD), 1) + i * BUILD, CAP)[0:1, :] + 1).astype(F32)
            weight = jnp.where(count_at == wanted, gate_at, 0.0)
            for q in range(ROWS // BUILD):
                acc_up[rows_at(i, BUILD), q * BUILD : (q + 1) * BUILD] = weight[
                    q * BUILD : (q + 1) * BUILD, :
                ]

    @pl.loop(0, FLAT_FIRST)
    def _(k):
        flat_node_send(k)

    @pl.loop(0, TYPES)
    def _(t):
        there = (node, partner_at(t))
        send(named, named_in.at[t], sem_named.at[0, t], sem_named.at[1, t], there)

    @pl.loop(FLAT_FIRST, chunks)
    def _(k):
        there = (node, partner_at(k))
        send(
            tok.at[:, columns(k)], shared.at[k], sem_shared.at[0, k], sem_shared.at[1, k], there
        )

    gates[0, rows_at(node, NODE_ROWS), :] = gate_out[rows_at(node, NODE_ROWS), :]

    node_send(FLAT_FIRST)
    wait_for(gates.at[0, pl.ds(0, (NODES - 1) * NODE_ROWS)], sem_misc.at[1])

    @pl.loop(0, TYPES)
    def _(t):
        there = (node, partner_at(t))
        send(gates.at[0], gates.at[1 + t], sem_gates.at[0, t], sem_gates.at[1, t], there)

    count_rows(0)
    build_flat_pick()

    @pl.loop(FLAT_FIRST + 1, AHEAD)
    def _(k):
        node_send(k)

    lat_rows = LOCALS * NODES * 2

    def latent_first():
        width = latent_cache.shape[0]
        lat_pad[0:width, :] = lat_t[...]
        lat_pad[width:, :] = ones_where(iota((LAT_PAD - width, TOK), 0) == 0).astype(BF16)
        row = iota((lat_rows, TOK), 0)
        owner_of_row = (((row & 15) >> 1) << 4) + (row >> 4)
        owned = ones_where(owner[...] == owner_of_row)
        upto = ones_where(iota((TOK, TOK), 0) <= iota((TOK, TOK), 1)).astype(BF16)
        rank = mm(owned.astype(BF16), upto)
        lat_pick = jnp.where(rank == ((row & 1) + 1).astype(F32), owned, 0.0).astype(BF16)
        lat_s1[...] = mm_nt(lat_pick, lat_pad[...]).astype(BF16)
        to_locals(lat_s1, lat_r1, 16, sem_misc.at[2], sem_misc.at[3])
        lat_r1[rows_at(local, 16), :] = lat_s1[rows_at(local, 16), :]

    def latent_second():
        wait_for(lat_r1.at[pl.ds(0, lat_rows - 16)], sem_misc.at[3])
        row = iota((lat_rows, lat_rows), 0)
        source = (((row & 31) >> 1) << 4) + ((row >> 5) << 1) + (row & 1)
        turn = ones_where(iota((lat_rows, lat_rows), 1) == source).astype(BF16)
        lat_s2[...] = mm(turn, lat_r1[...]).astype(BF16)
        to_nodes(lat_s2, lat_r2, 32, sem_misc.at[4], sem_misc.at[5])
        lat_r2[rows_at(node, 32), :] = lat_s2[rows_at(node, 32), :]

    def latent_third():
        wait_for(lat_r2.at[pl.ds(0, lat_rows - 32)], sem_misc.at[5])
        arrived = lat_r2[...]
        mark = ones_where(iota((8, LAT_PAD), 1) == latent_cache.shape[0]).astype(BF16)
        live = mm_nt(mark, arrived)
        upto = ones_where(iota((lat_rows, lat_rows), 0) <= iota((lat_rows, lat_rows), 1))
        place = mm(live.astype(BF16), upto.astype(BF16))
        wanted = (iota((TOK, lat_rows), 0) + 1).astype(F32)
        settle = jnp.where(place[0:1, :] == wanted, live[0:1, :], 0.0).astype(BF16)
        settled = jnp.transpose(mm(settle, arrived))
        latent_cache[...] = settled[0 : latent_cache.shape[0], :].astype(BF16)

    def wait_group(k, cy):
        py, _ = partner_of(y, x, k)
        pairs = (k >= FLAT_FIRST) & (cy == py)
        missing = (cy == y).astype(jnp.int32) + pairs.astype(jnp.int32)
        for skipped in range(3):

            @pl.when(missing == skipped)
            def _():
                wait_for(rx.at[k, pl.ds(0, GROUP - skipped * CAP)], sem_rx.at[k, cy])

    def expert_in(k):
        for copy in weights_in(k):
            copy.wait()
        slot = lax.rem(k, 2)

        @pl.loop(0, SIDE)
        def _(g):
            cy = lax.rem(y + g, SIDE)
            wait_group(k, cy)
            rows = rows_at(cy, GROUP)
            part = rx[k, rows, :]

            @pl.when(k == 0)
            def _():
                acc_gate[rows, :] = mm(part, wg_buf[slot])
                acc_up[rows, :] = mm(part, wu_buf[slot])

            @pl.when(k > 0)
            def _():
                acc_gate[rows, :] += mm(part, wg_buf[slot])
                acc_up[rows, :] += mm(part, wu_buf[slot])

        @pl.when(k + 2 < chunks)
        def _():
            for copy in weights_in(k + 2):
                copy.start()

    def paired_rows(k):
        t = lax.rem(k, TYPES)
        slot = lax.rem(k, TX_SLOTS)

        @pl.when(k < FLAT_FIRST + TYPES)
        def _():
            wait_for(gates.at[1 + t], sem_gates.at[1, t])
            count_rows(1 + t)
            build_pick(t)

        wait_for(passed.at[k, pl.ds(0, (NODES - 1) * PAIR_ROWS)], sem_z.at[1, k])

        @pl.when(k >= TX_SLOTS)
        def _():
            old = k - TX_SLOTS
            wait_slots(old < FLAT_FIRST, tx.at[slot], sem_tx.at[old])

        for side in range(2):
            arrived = get_pair(passed, k, side)
            rows = pl.ds(side * HALF, HALF)
            tx[slot, rows, :] = mm(moves[t, side], arrived).astype(BF16)

        py, px = partner_of(y, x, k)

        @pl.loop(0, REMOTE)
        def _(m):
            side = m // (COVER - 1)
            i = 1 + lax.rem(m * STRIDE, COVER - 1)
            ey, ex = cover(k, i // SIDE, lax.rem(i, SIDE))
            cy = y + side * (py - y)
            cx = x + side * (px - x)
            send(
                tx.at[slot, rows_at(side * COVER + i, CAP)],
                rx.at[k, rows_at(cy * SIDE + cx, CAP)],
                sem_tx.at[k],
                sem_rx.at[k, cy],
                (node, ey * SIDE + ex),
            )

        rx[k, rows_at(local, CAP), :] = tx[slot, 0:CAP, :]
        rx[k, rows_at(py * SIDE + px, CAP), :] = tx[slot, HALF : HALF + CAP, :]

    def flat_rows(k):
        wait_for(passed.at[k, pl.ds(0, (NODES - 1) * NODE_ROWS)], sem_z.at[1, k])
        tx[k] = mm(hidden[:, 0:ROWS], passed[k, 0:ROWS, :]).astype(BF16)

        @pl.loop(1, LOCALS)
        def _(d):
            peer = local_peer(lax.rem(d * STRIDE, LOCALS))
            send(
                tx.at[k, rows_at(peer, CAP)],
                rx.at[k, rows_at(local, CAP)],
                sem_tx.at[k],
                sem_rx.at[k, y],
                (node, peer),
            )

        rx[k, rows_at(local, CAP), :] = tx[k, rows_at(local, CAP), :]

    @pl.loop(0, chunks - 1 + EXPERT_LAG)
    def _(k):
        @pl.when(k < FLAT_FIRST)
        def _():
            flat_rows(k)

        @pl.when((k >= FLAT_FIRST) & (k < chunks))
        def _():
            paired_rows(k)

        @pl.when(k + AHEAD < chunks)
        def _():
            node_send(k + AHEAD)

        @pl.when(k == 4)
        def _():
            latent_first()

        @pl.when(k == 8)
        def _():
            latent_second()

        @pl.when(k >= EXPERT_LAG)
        def _():
            expert_in(k - EXPERT_LAG)

    def send_back(k, a, b, side):
        fy, fx = cover(k, a, b)
        py, px = partner_of(fy, fx, k)
        cy = fy + side * (py - fy)
        cx = fx + side * (px - fx)
        i = a * SIDE + lax.rem(SIDE - b, SIDE)
        send(
            rx.at[k, rows_at(cy * SIDE + cx, CAP)],
            passed.at[k, rows_at(side * COVER + i, CAP)],
            sem_ret.at[0, k],
            sem_ret.at[1, k],
            (node, fy * SIDE + fx),
        )

    def keep_back(k):
        passed[k, 0:CAP, :] = rx[k, rows_at(local, CAP), :]
        passed[k, HALF : HALF + CAP, :] = rx[k, rows_at(partner_at(k), CAP), :]

    last = chunks - 1
    for copy in weights_in(last):
        copy.wait()
    down_in(0).wait()

    @pl.loop(0, SIDE)
    def _(g):
        a, side = lax.rem(g, 2), g // 2
        fy, fx = cover(0, a, 0)
        py, _ = partner_of(fy, fx, 0)
        there = fy + side * (py - fy)
        wait_group(last, there)
        rows = rows_at(there, GROUP)
        part = rx[last, rows, :]
        gate_act = acc_gate[rows, :] + mm(part, wg_buf[last % 2])
        up_act = acc_up[rows, :] + mm(part, wu_buf[last % 2])
        hidden[rows, :] = (gate_act / (1.0 + jnp.exp(-gate_act)) * up_act).astype(BF16)
        rx[0, rows, :] = mm(hidden[rows, :], wd_buf[0]).astype(BF16)

        @pl.loop(0, SIDE)
        def _(b):
            @pl.when(a + b > 0)
            def _():
                send_back(0, a, b, side)

    keep_back(0)
    down_in(2).start()

    @pl.loop(chunks - ZS_SLOTS, chunks)
    def _(k):
        wait_for(zs.at[0, pl.ds(0, (NODES - 1) * PAIR_ROWS)], sem_z.at[0, k])

    @pl.loop(chunks - TX_SLOTS, chunks)
    def _(k):
        wait_for(tx.at[0, pl.ds(0, REMOTE * CAP)], sem_tx.at[k])

    parts = [pl.ds(i * BUILD, BUILD) for i in range(HALF // BUILD)]

    def node_part(k):
        t = lax.rem(k, TYPES)
        slot = lax.rem(k, ZS_SLOTS)

        @pl.when(k < TYPES)
        def _():
            build_combine(t)

        wait_for(passed.at[k, pl.ds(0, REMOTE * CAP)], sem_ret.at[1, k])

        @pl.when(k >= ZS_SLOTS)
        def _():
            old = k - ZS_SLOTS
            wait_node_rows(old >= flat_back, zs.at[slot], sem_back.at[0, old])

        for side in range(2):
            weight = jnp.concatenate(
                [
                    jnp.concatenate(
                        [moves[t, side, part, pl.ds(q * BUILD, BUILD)] for part in parts], axis=1
                    )
                    for q in range(ROWS // BUILD)
                ],
                axis=0,
            )
            total = mm(weight, passed[k, side * HALF : (side + 1) * HALF, :])
            put_pair(slot, side, total.astype(BF16))

        to_nodes(zs.at[slot], back.at[k], PAIR_ROWS, sem_back.at[0, k], sem_back.at[1, k])
        back[k, rows_at(node, PAIR_ROWS), :] = zs[slot, rows_at(node, PAIR_ROWS), :]

    flat_parts = [pl.ds(i * BUILD, BUILD) for i in range(SLOTS // BUILD)]

    def flat_part(k):
        slot = lax.rem(k, ZS_SLOTS)
        wait_for(passed.at[k, pl.ds(0, (LOCALS - 1) * CAP)], sem_ret.at[1, k])
        old = k - ZS_SLOTS
        wait_node_rows(old >= flat_back, zs.at[slot], sem_back.at[0, old])
        for q in range(ROWS // BUILD):
            weight = jnp.concatenate(
                [acc_up[part, pl.ds(q * BUILD, BUILD)] for part in flat_parts], axis=1
            ).astype(BF16)
            zs[slot, q * BUILD : (q + 1) * BUILD, :] = mm(weight, passed[k]).astype(BF16)
        to_nodes(zs.at[slot], back.at[k], NODE_ROWS, sem_back.at[0, k], sem_back.at[1, k])
        back[k, rows_at(node, NODE_ROWS), :] = zs[slot, rows_at(node, NODE_ROWS), :]

    def flat_finish(k):
        wait_for(back.at[k, pl.ds(0, (NODES - 1) * NODE_ROWS)], sem_back.at[1, k])
        moe[:, columns(k)] = mm(choose_t[0], back[k, 0:ROWS, :]).astype(BF16)

    def to_partner(k):
        t = lax.rem(k, TYPES)

        @pl.when(k < TYPES)
        def _():
            choose_t[1 + t] = jnp.transpose(choose[1 + t].astype(F32)).astype(BF16)

        wait_for(back.at[k, pl.ds(0, (NODES - 1) * PAIR_ROWS)], sem_back.at[1, k])
        shared[k] = mm(choose_t[1 + t], get_pair(back, k, 1)).astype(BF16)
        there = (node, partner_at(k))
        send(shared.at[k], shared_back.at[k], sem_home.at[0, k], sem_home.at[1, k], there)

    def finish(k):
        own = mm(choose_t[0], get_pair(back, k, 0))
        wait_for(shared_back.at[k], sem_home.at[1, k])
        moe[:, columns(k)] = (own + shared_back[k].astype(F32)).astype(BF16)

    choose_t[0] = jnp.transpose(choose[0].astype(F32)).astype(BF16)

    @pl.loop(1, chunks + END_LAG)
    def _(k):
        @pl.when(k < chunks)
        def _():
            slot = lax.rem(k, 2)
            down_in(k).wait()

            @pl.loop(0, SIDE)
            def _(i):
                rows = rows_at(i, GROUP)
                rx[k, rows, :] = mm(hidden[rows, :], wd_buf[slot]).astype(BF16)

            @pl.when(k < flat_back)
            def _():
                @pl.loop(0, REMOTE)
                def _(m):
                    j = 1 + lax.rem(m * STRIDE, COVER - 1)
                    send_back(k, j // SIDE, lax.rem(j, SIDE), m // (COVER - 1))

                keep_back(k)

            @pl.when(k >= flat_back)
            def _():
                to_locals(rx.at[k], passed.at[k], CAP, sem_ret.at[0, k], sem_ret.at[1, k])
                passed[k, rows_at(local, CAP), :] = rx[k, rows_at(local, CAP), :]

            @pl.when(k + 2 < chunks)
            def _():
                down_in(k + 2).start()

        @pl.when((k >= PART_LAG) & (k < flat_back + PART_LAG))
        def _():
            node_part(k - PART_LAG)

        @pl.when((k >= flat_back + PART_LAG) & (k < chunks + PART_LAG))
        def _():
            flat_part(k - PART_LAG)

        @pl.when(k == 10)
        def _():
            build_flat_combine()

        @pl.when(k == 9)
        def _():
            latent_third()

        @pl.when((k >= HOME_LAG) & (k < flat_back + HOME_LAG))
        def _():
            to_partner(k - HOME_LAG)

        @pl.when((k >= END_LAG) & (k < flat_back + END_LAG))
        def _():
            finish(k - END_LAG)

        @pl.when(k >= flat_back + END_LAG)
        def _():
            flat_finish(k - END_LAG)

    @pl.loop(FLAT_FIRST, chunks)
    def _(k):
        wait_for(shared.at[k], sem_shared.at[0, k])

    @pl.loop(0, chunks)
    def _(k):
        wait_slots(k >= flat_back, rx.at[k], sem_ret.at[0, k])

    @pl.loop(0, flat_back)
    def _(k):
        wait_for(shared.at[k], sem_home.at[0, k])

    @pl.loop(chunks - ZS_SLOTS, chunks)
    def _(k):
        wait_node_rows(k >= flat_back, zs.at[0], sem_back.at[0, k])

    @pl.loop(0, TYPES)
    def _(t):
        wait_for(named, sem_named.at[0, t])
        wait_for(gates.at[0], sem_gates.at[0, t])

    wait_for(gate_out.at[pl.ds(0, (NODES - 1) * NODE_ROWS)], sem_misc.at[0])
    wait_for(lat_s1.at[pl.ds(0, lat_rows - 16)], sem_misc.at[2])
    wait_for(lat_s2.at[pl.ds(0, lat_rows - 32)], sem_misc.at[4])


def per_device(tokens, ids, weights, wg, wu, wd, latent_rows, latent_owner):
    count, width = tokens.shape
    lat_width = latent_rows.shape[1]
    hidden_width = wg.shape[2]
    chunks = width // WIDTH
    vmem = pl.BlockSpec(memory_space=pltpu.VMEM)
    hbm = pl.BlockSpec(memory_space=pl.ANY)
    lat_all = LOCALS * NODES * 2
    dma = pltpu.SemaphoreType.DMA
    moe, cache_t = pl.pallas_call(
        functools.partial(kernel, chunks),
        out_shape=(
            jax.ShapeDtypeStruct((count, width), BF16),
            jax.ShapeDtypeStruct((lat_width, count), BF16),
        ),
        in_specs=[vmem] * 5 + [hbm] * 3,
        out_specs=(vmem, vmem),
        scratch_shapes=[
            pltpu.VMEM((2 * ids.shape[1], TOK), F32),
            pltpu.VMEM((TYPES, 2 * ids.shape[1], TOK), F32),
            pltpu.VMEM((1 + TYPES, ROWS, TOK), BF16),
            pltpu.VMEM((1 + TYPES, TOK, ROWS), BF16),
            pltpu.VMEM((1 + TYPES, ROWS, TOK), BF16),
            pltpu.VMEM((1 + TYPES, ROWS, TOK), BF16),
            pltpu.VMEM((ROWS, TOK), BF16),
            pltpu.VMEM((TYPES, 2, HALF, ROWS), BF16),
            pltpu.VMEM((chunks, TOK, WIDTH), BF16),
            pltpu.VMEM((chunks, TOK, WIDTH), BF16),
            pltpu.VMEM((ZS_SLOTS, NODES * PAIR_ROWS, WIDTH), BF16),
            pltpu.VMEM((chunks, SLOTS, WIDTH), BF16),
            pltpu.VMEM((TX_SLOTS, SLOTS, WIDTH), BF16),
            pltpu.VMEM((chunks, SLOTS, WIDTH), BF16),
            pltpu.VMEM((chunks, NODES * PAIR_ROWS, WIDTH), BF16),
            pltpu.VMEM((SLOTS, hidden_width), F32),
            pltpu.VMEM((SLOTS, hidden_width), F32),
            pltpu.VMEM((SLOTS, hidden_width), BF16),
            pltpu.VMEM((2, WIDTH, hidden_width), BF16),
            pltpu.VMEM((2, WIDTH, hidden_width), BF16),
            pltpu.VMEM((2, hidden_width, WIDTH), BF16),
            pltpu.VMEM((LAT_PAD, count), BF16),
            pltpu.VMEM((lat_all, LAT_PAD), BF16),
            pltpu.VMEM((lat_all, LAT_PAD), BF16),
            pltpu.VMEM((lat_all, LAT_PAD), BF16),
            pltpu.VMEM((lat_all, LAT_PAD), BF16),
            dma((3, 2)),
            dma((2, TYPES)),
            dma((2, TYPES)),
            dma((2, chunks)),
            dma((2, chunks)),
            dma((2, chunks)),
            dma((chunks,)),
            dma((chunks, SIDE)),
            dma((2, chunks)),
            dma((2, chunks)),
            dma((6,)),
        ],
        compiler_params=pltpu.CompilerParams(
            collective_id=0, has_side_effects=True, vmem_limit_bytes=62 * 2**20
        ),
        cost_estimate=pl.CostEstimate(
            flops=6 * SLOTS * width * hidden_width,
            bytes_accessed=6 * width * hidden_width,
            transcendentals=SLOTS * hidden_width,
        ),
        name="moe_exchange",
    )(
        tokens,
        jnp.transpose(ids),
        jnp.transpose(weights),
        jnp.transpose(latent_rows),
        latent_owner.reshape(1, count),
        wg,
        wu,
        wd,
    )
    return moe, jnp.transpose(cache_t)


def solution(mesh):
    rows = P(("node", "local"), None)
    experts = P(("node", "local"), None, None)
    return jax.shard_map(
        per_device,
        mesh=mesh,
        in_specs=(rows, rows, rows, experts, experts, experts, rows, P(("node", "local"))),
        out_specs=(rows, rows),
        check_vma=False,
    )
```
